512 devices in a mesh: lon: 32 (over y, x, core), lat: 8 (over z_lo), depth: 2 (over z_hi).
Axes of the slice: x: 4, y: 4, z: 16 (z_hi: 2, z_lo: 8; z = z_hi * 8 + z_lo), core: 2. Of those that a mesh axis runs over, the one named last changes fastest.
Arguments:
- adj_temp: float32 [96, 64, 4096], P('depth', 'lat', 'lon'), may hold values from -6 to 6
- adj_salt: float32 [96, 64, 4096], P('depth', 'lat', 'lon'), may hold values from -6 to 6
- adj_zonal: float32 [96, 64, 4096], P('depth', 'lat', 'lon'), may hold values from -6 to 6
- adj_merid: float32 [96, 64, 4096], P('depth', 'lat', 'lon'), may hold values from -6 to 6
- east_speed: float32 [96, 64, 4096], P('depth', 'lat', 'lon'), may hold values from -4 to 4
- north_speed: float32 [96, 64, 4096], P('depth', 'lat', 'lon'), may hold values from -4 to 4
- branch_flags: int32 [2, 96, 64, 4096], P(None, 'depth', 'lat', 'lon'), may hold values from 0 to 8
- sea_mask: int32 [96, 64, 4096], P('depth', 'lat', 'lon'), may hold values 0 or 1
- block_inverse: float32 [64, 96, 48], P('lat', 'depth'), may hold values from -1 to 1, as said below
- coupling: float32 [64], P('lat'), may hold values from 0.3 to 0.9
Outputs:
- grad_temp: float32 [96, 64, 4096], P('depth', 'lat', 'lon')
- grad_salt: float32 [96, 64, 4096], P('depth', 'lat', 'lon')
- grad_zonal: float32 [96, 64, 4096], P('depth', 'lat', 'lon')
- grad_merid: float32 [96, 64, 4096], P('depth', 'lat', 'lon')
The draws below stay inside these ranges and needn't reach their ends.
Inputs may be any that keep to these rules, and one draw needn't show every extreme that they name: `branch_flags`: a flag is 3 times the branch of the north face plus the branch of the east face. `sea_mask`: 1 marks a sea cell. `block_inverse`: the diagonal entries of every 48 x 48 block lie between 0.4 and 1, the other entries between -0.5 / 48 and 0.5 / 48.
All inputs are finite; a program needn't handle non-finite values. No bound on the sum of `sea_mask` on one device may be relied on, other than what follows from the above.
Results may differ from the reference program's by a relative error of at most 0.00016.
Values sent between devices are 32-bit elements; how exact they have to be, the bound alone decides.
A program may use at most 64 MiB of HBM per device.

```python
import math
import jax
import jax.numpy as jnp
from jax import lax

LEV_DEV = 48
STEPS = 2
NX = 4096
NY = 64
LEVELS = 96


def draw_block_inverse(key, part):
    key_diag, key_off = jax.random.split(jax.random.fold_in(key, 7))
    rows_pos = jnp.arange(LEVELS)[:, None] % LEV_DEV
    cols_pos = jnp.arange(LEV_DEV)[None, :]
    on_diag = (rows_pos == cols_pos)[None]
    diagonal = jax.random.uniform(key_diag, (NY, LEVELS, LEV_DEV), jnp.float32, 0.5, 0.9)
    others = jnp.clip(jax.random.normal(key_off, (NY, LEVELS, LEV_DEV), jnp.float32), -1.6, 1.6) * (0.3 / LEV_DEV)
    return jnp.where(on_diag, diagonal, others)


def place_ends(result, stream_key, smallest, top_value):
    longest = result.shape.index(max(result.shape))
    spots = []
    for shift in (0, 1):
        where = [jax.random.randint(jax.random.fold_in(stream_key, axis), (), 0, length) for axis, length in enumerate(result.shape)]
        where[longest] = (where[longest] + shift) % result.shape[longest]
        spots.append(tuple(where))
    return result.at[spots[0]].set(smallest).at[spots[1]].set(top_value)


def levels(own_key, extent, shards, low, top_value):
    level = 1.0
    for axis_at, parts in shards:
        steps = jax.random.uniform(jax.random.fold_in(jax.random.fold_in(own_key, 6), axis_at), (parts,), jnp.float32, low / len(shards), top_value / len(shards))
        level = level * jnp.repeat(jnp.exp(steps), extent[axis_at] // parts).reshape((-1,) + (1,) * (len(extent) - 1 - axis_at))
    return level


def centred(own_key, shape, scale, bound, cuts=(), held_as=jnp.bfloat16):
    level = levels(own_key, shape, cuts, -0.22, 0.18) if cuts else 1.0
    result = jax.random.normal(own_key, shape, jnp.float32) * scale * level
    return jnp.minimum(jnp.maximum(result, -bound), bound).astype(held_as)


def setup_inputs(seed: int = 0) -> dict:
    keys = jax.random.split(jax.random.key(seed), 11)
    return {
        "adj_temp": centred(keys[0], (LEVELS, NY, NX), 1.0, 6.0, ((0, 2), (1, 8), (2, 32)), jnp.float32),
        "adj_salt": centred(keys[1], (LEVELS, NY, NX), 1.0, 6.0, ((0, 2), (1, 8), (2, 32)), jnp.float32),
        "adj_zonal": centred(keys[2], (LEVELS, NY, NX), 1.0, 6.0, ((0, 2), (1, 8), (2, 32)), jnp.float32),
        "adj_merid": centred(keys[3], (LEVELS, NY, NX), 1.0, 6.0, ((0, 2), (1, 8), (2, 32)), jnp.float32),
        "east_speed": centred(keys[4], (LEVELS, NY, NX), 1.0, 4.0, ((0, 2), (1, 8), (2, 32)), jnp.float32),
        "north_speed": centred(keys[5], (LEVELS, NY, NX), 0.7, 4.0, ((0, 2), (1, 8), (2, 32)), jnp.float32),
        "branch_flags": place_ends(jax.random.randint(keys[6], (STEPS, LEVELS, NY, NX), 0, 9), jax.random.fold_in(keys[6], 1), 0, 8).astype(jnp.int32),
        "sea_mask": place_ends((jax.random.randint(keys[7], (LEVELS, NY, NX), 0, 6) < 5).astype(jnp.int32), jax.random.fold_in(keys[7], 1), 0, 1),
        "block_inverse": draw_block_inverse(jax.random.fold_in(keys[10], 71), 0),
        "coupling": jnp.clip(jnp.exp(math.log(0.9) - 1.0986122 * jax.random.uniform(keys[9], (NY,), jnp.float32) ** levels(keys[9], (NY,), ((0, 8),), -0.2, 0.2)), 0.3, 0.9),
    }


advect_scale = 0.25
diffusion = 0.5
gravity = 0.1
pressure_scale = 1.0
viscosity = 0.1
haline = 0.8

def eastward(field):
    return jnp.roll(field, -1, axis=2)

def westward(field):
    return jnp.roll(field, 1, axis=2)

def northward(field):
    return jnp.concatenate([field[:, 1:, :], jnp.zeros_like(field[:, :1, :])], axis=1)

def southward(field):
    return jnp.concatenate([jnp.zeros_like(field[:, :1, :]), field[:, :-1, :]], axis=1)

def laplace(field):
    return eastward(field) + westward(field) + northward(field) + southward(field) - 4.0 * field

def column_solve(field, block_inverse, coupling):
    upper_block = block_inverse[:, :LEV_DEV, :]
    lower_block = block_inverse[:, LEV_DEV:, :]
    highest = lax.Precision.HIGHEST
    upper_part = jnp.einsum('yjk,kyx->jyx', upper_block, field[:LEV_DEV], precision=highest)
    lower_part = jnp.einsum('yjk,kyx->jyx', lower_block, field[LEV_DEV:], precision=highest)
    upper_corner = upper_block[:, LEV_DEV - 1, LEV_DEV - 1]
    lower_corner = lower_block[:, 0, 0]
    divisor = (1.0 - coupling * coupling * upper_corner * lower_corner)[:, None]
    first = upper_part[LEV_DEV - 1]
    second = lower_part[0]
    upper_value = (first + (coupling * upper_corner)[:, None] * second) / divisor
    lower_value = (second + (coupling * lower_corner)[:, None] * first) / divisor
    upper_part = upper_part + (coupling[:, None] * upper_block[:, :, LEV_DEV - 1]).T[:, :, None] * lower_value[None]
    lower_part = lower_part + (coupling[:, None] * lower_block[:, :, 0]).T[:, :, None] * upper_value[None]
    return jnp.concatenate([upper_part, lower_part], axis=0)

def forward_step(state, flags_now, east_speed, north_speed, sea, block_inverse, coupling):
    zonal_branch = (flags_now % 3).astype(jnp.float32) * 0.5
    merid_branch = (flags_now // 3).astype(jnp.float32) * 0.5
    east_open = sea * eastward(sea)
    north_open = sea * northward(sea)
    east_self = east_open * (east_speed * (1.0 - zonal_branch) + diffusion)
    east_next = east_open * (east_speed * zonal_branch - diffusion)
    north_self = north_open * (north_speed * (1.0 - merid_branch) + diffusion)
    north_next = north_open * (north_speed * merid_branch - diffusion)

    def tracer(field):
        flux_east = east_self * field + east_next * eastward(field)
        flux_north = north_self * field + north_next * northward(field)
        return sea * (field - advect_scale * (flux_east - westward(flux_east) + flux_north - southward(flux_north)))
    temp, salt, zonal, merid = state
    pressure = gravity * jnp.cumsum(temp - haline * salt, axis=0)
    coriolis = (0.2 + 0.6 * (jnp.arange(NY).astype(jnp.float32) + 0.5) / NY)[None, :, None]
    zonal_star = sea * (zonal + coriolis * merid - 0.5 * pressure_scale * (eastward(pressure) - westward(pressure)) + viscosity * laplace(zonal))
    merid_star = sea * (merid - coriolis * zonal - 0.5 * pressure_scale * (northward(pressure) - southward(pressure)) + viscosity * laplace(merid))
    return (column_solve(tracer(temp), block_inverse, coupling), column_solve(tracer(salt), block_inverse, coupling), column_solve(zonal_star, block_inverse, coupling), column_solve(merid_star, block_inverse, coupling))

def reference(adj_temp, adj_salt, adj_zonal, adj_merid, east_speed, north_speed, branch_flags, sea_mask, block_inverse, coupling):
    sea = sea_mask.astype(jnp.float32)
    state = (adj_temp, adj_salt, adj_zonal, adj_merid)
    zeros = (jnp.zeros_like(adj_temp), jnp.zeros_like(adj_temp), jnp.zeros_like(adj_temp), jnp.zeros_like(adj_temp))
    for step_index in reversed(range(STEPS)):
        flags_now = branch_flags[step_index]

        def advance(temp, salt, zonal, merid):
            return forward_step((temp, salt, zonal, merid), flags_now, east_speed, north_speed, sea, block_inverse, coupling)
        outputs, pullback = jax.vjp(advance, *zeros)
        state = pullback(state)
    return (state[0], state[1], state[2], state[3])
```

```python
import functools

import jax
import jax.numpy as jnp
from jax import lax
from jax.experimental import pallas as pl
from jax.experimental.pallas import tpu as pltpu
from jax.sharding import PartitionSpec as P

MESH = pl.DeviceIdType.MESH
F32, BF16, I32 = jnp.float32, jnp.bfloat16, jnp.int32

STEPS = 2
advect_scale = 0.25
diffusion = 0.5
gravity = 0.1
pressure_scale = 1.0
viscosity = 0.1
haline = 0.8

CORNER, PLANE, ZU, ZV, ZS = 0, 1, 5, 6, 7
LOW, HIGH = 0, 1
DEP, LON, LAT, DLON, DLAT, COEF, MISC = 0, 1, 3, 5, 7, 9, 11


def tile(k):
    return pl.ds(pl.multiple_of(k * 8, 8), 8)


def split(value):
    high = value.astype(BF16)
    return high, (value - high.astype(F32)).astype(BF16)


def kernel(
    n_lon, n_lat, lev,
    a_t, a_s, a_u, a_v, es_h, ns_h, fl_h, sea_h, inv_h, coup_h,
    out,
    st, es, ns, fl, sea_i, inv,
    sea, cs, sh, e_own, w_own, n_own, s_own, c0, proj, hx, enh, w3,
    wlat, cs_lat, spike,
    d_s, d_r, lon_s, lon_r, lat_s, lat_r, coef_s, coef_r, misc_s, misc_r, dl_s, dl_r, dt_s, dt_r,
    coup, in_sem, send_sem, recv_sem,
):
    lon, lat, dep = lax.axis_index("lon"), lax.axis_index("lat"), lax.axis_index("depth")
    edge = (lev - 1) * (1 - dep)
    cells = lev * 8
    east, west = lax.rem(lon + 1, n_lon), lax.rem(lon + n_lon - 1, n_lon)
    has_low, has_high = lat > 0, lat < n_lat - 1
    other = 1 - dep

    loads = []
    for i, (src, dst) in enumerate(
        [(inv_h, inv), (a_t, st.at[0]), (a_s, st.at[1]), (a_u, st.at[2]), (a_v, st.at[3]),
         (sea_h, sea_i), (es_h, es), (ns_h, ns), (fl_h, fl), (coup_h, coup)]
    ):
        copy = pltpu.make_async_copy(src, dst, in_sem.at[i])
        copy.start()
        loads.append(copy)

    barrier = pltpu.get_barrier_semaphore()

    def greet(device):
        pl.semaphore_signal(barrier, inc=1, device_id=device, device_id_type=MESH)

    greet((lon, lat, other))
    for depth in (other, dep):
        greet((east, lat, depth))
        greet((west, lat, depth))

        @pl.when(has_low)
        def _():
            greet((lon, lat - 1, depth))

        @pl.when(has_high)
        def _():
            greet((lon, lat + 1, depth))

    lane = lax.broadcasted_iota(I32, (8, 128), 1)
    sub = lax.broadcasted_iota(I32, (8, 128), 0)
    first_lane, last_lane = lane == 0, lane == 127
    first_sub, last_sub = sub == 0, sub == 7
    zero = jnp.zeros((8, 128), F32)

    def to_east(a, halo):
        return jnp.where(last_lane, halo, pltpu.roll(a, 127, 1))

    def to_west(a, halo):
        return jnp.where(first_lane, halo, pltpu.roll(a, 1, 1))

    def to_north(a, halo):
        return jnp.where(last_sub, halo, pltpu.roll(a, 7, 0))

    def to_south(a, halo):
        return jnp.where(first_sub, halo, pltpu.roll(a, 1, 0))

    def copies(step):
        def remote(slot, src, dst, device):
            return pltpu.make_async_remote_copy(
                src_ref=src, dst_ref=dst, send_sem=send_sem.at[step, slot],
                recv_sem=recv_sem.at[step, slot], device_id=device, device_id_type=MESH,
            )

        first = step == 0
        upward = pl.ds(0, 8) if first else pl.ds(1, 6)
        downward = pl.ds(0, 5) if first else pl.ds(1, 4)
        todo = {}
        todo["up"] = (remote(DEP, d_s.at[step, upward], d_r.at[step, upward], (lon, lat, other)), dep == 1, dep == 0)
        todo["down"] = (remote(DEP, d_s.at[step, downward], d_r.at[step, downward], (lon, lat, other)), dep == 0, dep == 1)
        for side in (LOW, HIGH):
            far = 1 - side
            beside = east if side == HIGH else west
            row = lat + 1 if side == HIGH else lat - 1
            sends, gets = (has_high, has_low) if side == HIGH else (has_low, has_high)
            todo["dlon", side] = (remote(DLON + side, dl_s.at[step, side], dl_r.at[step, far], (beside, lat, other)), None, None)
            todo["dlat", side] = (remote(DLAT + side, dt_s.at[step, side], dt_r.at[step, far], (lon, row, other)), sends, gets)
            todo["lon", side] = (remote(LON + side, lon_s.at[step, side], lon_r.at[step, far], (beside, lat, dep)), None, None)
            todo["lat", side] = (remote(LAT + side, lat_s.at[step, side], lat_r.at[step, far], (lon, row, dep)), sends, gets)
            if first:
                count = 3 if side == HIGH else 1
                todo["coef", side] = (
                    remote(COEF + side, coef_s.at[side, pl.ds(0, count)], coef_r.at[far, pl.ds(0, count)], (lon, row, dep)), sends, gets)
                todo["misc", side] = (remote(MISC + side, misc_s, misc_r.at[far], (lon, row, dep)), sends, gets)
        return todo

    def act(entry, what):
        descriptor, sends, gets = entry
        call = {"start": descriptor.start, "send": descriptor.wait_send, "recv": descriptor.wait_recv}[what]
        condition = gets if what == "recv" else sends
        if condition is None:
            call()
        else:
            pl.when(condition)(call)

    for side, missing in ((LOW, lat == 0), (HIGH, lat == n_lat - 1)):

        @pl.when(missing)
        def _():
            for step in range(STEPS):
                lat_r[step, side] = jnp.zeros(lat_r.shape[2:], F32)
                dt_r[step, side] = zero
            coef_r[side] = jnp.zeros(coef_r.shape[1:], F32)
            misc_r[side] = jnp.zeros(misc_r.shape[1:], F32)

    loads[0].wait()
    loads[9].wait()
    coupling = zero
    for y in range(8):
        coupling = jnp.where(sub == y, coup[y], coupling)
    spike[...] = zero
    for y in range(8):
        spike[y : y + 1, 0:lev] = inv[y, pl.ds(edge, 1), :]
        high, low = split(inv[y])
        w3[y] = jnp.concatenate([high, high, low], axis=0)
    spike_rows = spike[...]
    corner = jnp.broadcast_to(
        jnp.sum(jnp.where(lane == edge, spike_rows, 0.0), axis=1, keepdims=True), (8, 128)
    )
    scaled = spike_rows * coupling
    for k in range(lev):
        cs[tile(k)] = jnp.broadcast_to(scaled[:, k : k + 1], (8, 128))
    misc_s[0] = scaled
    misc_s[1] = coupling
    misc_s[2] = corner

    def project(step):
        for y in range(8):
            rows = pl.ds(y, lev, stride=8)
            column = jnp.concatenate([st[f, rows, :] for f in range(4)], axis=1)
            high, low = split(column)
            stacked = jnp.concatenate([high, low, high], axis=0)
            result = lax.dot_general(
                w3[y], stacked, (((0,), (0,)), ((), ())), preferred_element_type=F32
            )
            for f in range(4):
                part = result[:, f * 128 : (f + 1) * 128]
                proj[f, rows, :] = part
                if y == 0:
                    lat_s[step, LOW, f] = part
                if y == 7:
                    lat_s[step, HIGH, f] = part

    for copy in loads[1:5]:
        copy.wait()
    project(0)

    for copy in loads[5:9]:
        copy.wait()

    def prepare(k, carry):
        t = tile(k)
        mask = sea_i[t].astype(F32)
        sea[t] = mask
        quarter = mask * advect_scale
        speed_e, speed_n = es[t], ns[t]
        for n in range(STEPS):
            flag = fl[n, t]
            third = lax.shift_right_logical(flag * 11, 5)
            zonal = (flag - 3 * third).astype(F32) * 0.5
            merid = third.astype(F32) * 0.5
            e_own[n, t] = quarter * (speed_e * (1.0 - zonal) + diffusion)
            w_own[n, t] = quarter * (speed_e * zonal - diffusion)
            n_own[n, t] = quarter * (speed_n * (1.0 - merid) + diffusion)
            s_own[n, t] = quarter * (speed_n * merid - diffusion)
        return carry + mask * cs[t]

    spike_sum = lax.fori_loop(0, lev, prepare, zero, unroll=4)
    d_s[0, CORNER] = corner
    d_s[0, ZS] = spike_sum
    for side, y in ((LOW, 0), (HIGH, 7)):
        rows = pl.ds(y, lev, stride=8)
        coef_s[side, 0] = sea[rows, :]
        if side == HIGH:
            for n in range(STEPS):
                coef_s[side, 1 + n] = s_own[n, rows, :]

    pick_row = lax.broadcasted_iota(I32, (16, 128), 0)
    pick_lane = lax.broadcasted_iota(I32, (16, 128), 1)
    pick_edge = pick_lane == jnp.where(pick_row < 8, 0, 127)

    def messages(step):
        planes = [proj[f, tile(edge)] for f in range(4)]

        def sums(k, carry):
            t = tile(k)
            return carry[0] + sea[t] * proj[2, t], carry[1] + sea[t] * proj[3, t]

        z_u, z_v = lax.fori_loop(0, lev, sums, (zero, zero), unroll=8)
        for f in range(4):
            d_s[step, PLANE + f] = planes[f]
        d_s[step, ZU] = z_u
        d_s[step, ZV] = z_v
        for side, x in ((LOW, 0), (HIGH, 127)):
            packed = zero
            for i, value in enumerate(planes + [z_u, spike_sum]):
                packed = jnp.where(lane == i, jnp.broadcast_to(value[:, x : x + 1], (8, 128)), packed)
            dl_s[step, side] = packed
        for side, y in ((LOW, 0), (HIGH, 7)):
            for i, value in enumerate([corner] + planes + [z_v, spike_sum]):
                dt_s[step, side, i : i + 1, :] = value[y : y + 1, :]
            dt_s[step, side, 7:8, :] = zero[0:1, :]

    def edges(step):
        fields = [proj.at[f] for f in range(4)]
        if step == 0:
            fields = fields + [sea, w_own.at[0], w_own.at[1]]
        total = jnp.zeros((16, cells), F32)
        for i, field in enumerate(fields):
            pick = jnp.where(pick_edge & (lax.rem(pick_row, 8) == i), 1.0, 0.0).astype(BF16)
            for part in split(field[...]):
                total += lax.dot_general(
                    pick, part, (((1,), (1,)), ((), ())), preferred_element_type=F32
                )
        lon_s[step, LOW] = total[0:8]
        lon_s[step, HIGH] = total[8:16]

    def spread(step):
        count = 7 if step == 0 else 4
        parts = []
        for side in (HIGH, LOW):
            value = lon_r[step, side]
            high = value.astype(BF16).astype(F32)
            parts += [high, value - high]
        stacked = jnp.concatenate(parts, axis=0).astype(BF16)
        row = lax.broadcasted_iota(I32, (32, 128), 0)
        at = lax.broadcasted_iota(I32, (32, 128), 1) == jnp.where(row < 16, 127, 0)
        place = jnp.concatenate(
            [jnp.where(at & (lax.rem(row, 8) == i), 1.0, 0.0) for i in range(count)], axis=1
        ).astype(BF16)
        wide = lax.dot_general(stacked, place, (((0,), (0,)), ((), ())), preferred_element_type=F32)
        for i, field in enumerate([hx.at[0], hx.at[1], hx.at[2], hx.at[3], sh, enh.at[0], enh.at[1]][:count]):
            field[...] = wide[:, i * 128 : (i + 1) * 128]

    def faces(k, carry):
        t = tile(k)
        mask, halo = sea[t], sh[t]
        row = pl.ds(k, 1)
        mask_e = to_east(mask, halo)
        mask_n = to_north(mask, coef_r[HIGH, 0, row, :])
        for n in range(STEPS):
            e = e_own[n, t] * mask_e
            w = mask * to_west(w_own[n, t], enh[n, t])
            north = n_own[n, t] * mask_n
            south = mask * to_south(s_own[n, t], coef_r[LOW, 1 + n, row, :])
            e_own[n, t] = e
            w_own[n, t] = w
            n_own[n, t] = north
            s_own[n, t] = south
            c0[n, t] = (1.0 - e + w) - (north - south)
        return carry

    def spread_spikes():
        k_at = lax.broadcasted_iota(I32, (lev, 128), 0)
        same = k_at == lax.broadcasted_iota(I32, (lev, 128), 1)
        for side, y in ((LOW, 7), (HIGH, 0)):
            row = misc_r[side, 0, y : y + 1, :]
            column = jnp.sum(jnp.where(same, jnp.broadcast_to(row, (lev, 128)), 0.0), axis=1, keepdims=True)
            cs_lat[side] = jnp.broadcast_to(column, (lev, 128))

    row_at = (sub + lat * 8).astype(F32)
    coriolis = 0.2 + 0.6 * (row_at + 0.5) / (8.0 * n_lat)

    def advance(step, n, target):
        other_corner = d_r[0, CORNER]
        alpha = 1.0 / (1.0 - coupling * coupling * corner * other_corner)
        beta = coupling * other_corner * alpha
        gamma = coupling * corner * alpha
        own = [proj[f, tile(edge)] for f in range(4)]
        far = [d_r[step, PLANE + f] for f in range(4)]
        carried = [alpha * far[f] + beta * own[f] for f in range(4)]

        def beside(i):
            low = jnp.broadcast_to(dl_r[step, LOW, :, i : i + 1], (8, 128))
            high = jnp.broadcast_to(dl_r[step, HIGH, :, i : i + 1], (8, 128))
            return jnp.where(last_lane, high, jnp.where(first_lane, low, 0.0))

        own_side = [hx[f, tile(edge)] for f in range(4)]
        far_side = [beside(f) for f in range(4)]
        carried_side = [alpha * far_side[f] + beta * own_side[f] for f in range(4)]

        z_u = d_r[step, ZU] + d_r[0, ZS] * (alpha * own[2] + gamma * far[2])
        z_v = d_r[step, ZV] + d_r[0, ZS] * (alpha * own[3] + gamma * far[3])
        z_side = beside(4) + beside(5) * (alpha * own_side[2] + gamma * far_side[2])
        z_rows = []
        for side, y in ((LOW, 7), (HIGH, 0)):
            c = misc_r[side, 1, y : y + 1, :]
            mine = misc_r[side, 2, y : y + 1, :]
            theirs = dt_r[step, side, 0:1, :]
            a = 1.0 / (1.0 - c * c * mine * theirs)
            b = c * theirs * a
            g = c * mine * a
            mask = coef_r[side, 0]
            for f in range(4):
                near = lat_r[step, side, f, pl.ds(edge, 1), :]
                row = dt_r[step, side, 1 + f : 2 + f, :]
                carried_row = a * row + b * near
                wlat[side, f] = mask * (lat_r[step, side, f] + cs_lat[side] * carried_row)
                if f == 3:
                    z_rows.append(dt_r[step, side, 5:6, :] + dt_r[step, side, 6:7, :] * (a * near + g * row))
        deeper = -0.5 * pressure_scale * (
            to_west(z_u, z_side) - to_east(z_u, z_side)
            + to_south(z_v, z_rows[LOW]) - to_north(z_v, z_rows[HIGH])
        )
        deeper = jnp.where(dep == 0, deeper, 0.0)

        def level(i, below):
            k = lev - 1 - i
            t = tile(k)
            row = pl.ds(k, 1)
            mask, tip, halo = sea[t], cs[t], sh[t]
            w, e_, w_, n_, s_ = [], [], [], [], []
            for f in range(4):
                here = mask * (proj[f, t] + tip * carried[f])
                side = halo * (hx[f, t] + tip * carried_side[f])
                w.append(here)
                e_.append(to_east(here, side))
                w_.append(to_west(here, side))
                n_.append(to_north(here, wlat[HIGH, f, row, :]))
                s_.append(to_south(here, wlat[LOW, f, row, :]))
            below = below + (-0.5 * pressure_scale) * (w_[2] - e_[2] + s_[3] - n_[3])
            lift = gravity * below
            ce, cw, cn, cs_, cc = e_own[n, t], w_own[n, t], n_own[n, t], s_own[n, t], c0[n, t]
            for f, part in ((0, lift), (1, -haline * lift)):
                target[f, t] = (cc * w[f] + ce * e_[f]) + (cn * n_[f] - cw * w_[f]) + (part - cs_ * s_[f])
            around = [e_[f] + w_[f] + n_[f] + s_[f] for f in (2, 3)]
            target[2, t] = (1.0 - 4.0 * viscosity) * w[2] - coriolis * w[3] + viscosity * around[0]
            target[3, t] = (1.0 - 4.0 * viscosity) * w[3] + coriolis * w[2] + viscosity * around[1]
            return below

        lax.fori_loop(0, lev, level, deeper, unroll=4)

    messages(0)
    edges(0)
    todo = [copies(0), copies(1)]
    pl.semaphore_wait(barrier, 5 + 2 * has_low.astype(I32) + 2 * has_high.astype(I32))

    for step in range(STEPS):
        now = todo[step]
        if step > 0:
            project(step)
            messages(step)
        order = ["up", "down"] + [(kind, side) for kind in ("dlat", "dlon") for side in (LOW, HIGH)]
        for name in order:
            act(now[name], "start")
        if step > 0:
            edges(step)
        rest = [(kind, side) for kind in ("lon", "misc", "coef", "lat") for side in (LOW, HIGH)]
        for name in rest:
            if name in now:
                act(now[name], "start")
        for name in rest:
            if name in now:
                act(now[name], "recv")
        spread(step)
        if step == 0:
            spread_spikes()
            lax.fori_loop(0, lev, faces, 0, unroll=4)
        for name in order:
            act(now[name], "recv")
        advance(step, STEPS - 1 - step, st if step < STEPS - 1 else out)
    for now in todo:
        for entry in now.values():
            act(entry, "send")


def store(state, *rest):
    outs, sem = rest[:4], rest[4]
    moves = [pltpu.make_async_copy(state.at[f], outs[f], sem.at[f]) for f in range(4)]
    for move in moves:
        move.start()
    for move in moves:
        move.wait()


def on_device(
    n_lon, n_lat,
    adj_temp, adj_salt, adj_zonal, adj_merid, east_speed, north_speed, branch_flags, sea_mask, block_inverse, coupling,
):
    lev, rows, cols = adj_temp.shape
    cells = lev * rows
    flat = [v.reshape(cells, cols) for v in (adj_temp, adj_salt, adj_zonal, adj_merid, east_speed, north_speed)]
    flags = branch_flags.reshape(STEPS, cells, cols)
    hbm = pl.BlockSpec(memory_space=pltpu.HBM)
    anywhere = pl.BlockSpec(memory_space=pl.ANY)
    vmem = pl.BlockSpec(memory_space=pltpu.VMEM)
    field = pltpu.VMEM((cells, cols), F32)

    def fields(*lead):
        return pltpu.VMEM((*lead, cells, cols), F32)

    def tiles(*lead):
        return pltpu.VMEM((*lead, 8, 128), F32)

    scratch = [
        fields(4), field, field, pltpu.VMEM((STEPS, cells, cols), I32), pltpu.VMEM((cells, cols), I32),
        pltpu.VMEM((rows, lev, lev), F32),
        field, field, field,
        fields(STEPS), fields(STEPS), fields(STEPS), fields(STEPS), fields(STEPS),
        fields(4), fields(4), fields(STEPS), pltpu.VMEM((rows, 3 * lev, lev), BF16),
        pltpu.VMEM((2, 4, lev, 128), F32), pltpu.VMEM((2, lev, 128), F32), tiles(),
        tiles(STEPS, 8), tiles(STEPS, 8),
        pltpu.VMEM((STEPS, 2, 8, cells), F32), pltpu.VMEM((STEPS, 2, 8, cells), F32),
        pltpu.VMEM((STEPS, 2, 4, lev, 128), F32), pltpu.VMEM((STEPS, 2, 4, lev, 128), F32),
        pltpu.VMEM((2, 3, lev, 128), F32), pltpu.VMEM((2, 3, lev, 128), F32),
        tiles(3), tiles(2, 3),
        tiles(STEPS, 2), tiles(STEPS, 2), tiles(STEPS, 2), tiles(STEPS, 2),
        pltpu.SMEM((rows,), F32), pltpu.SemaphoreType.DMA((10,)),
        pltpu.SemaphoreType.DMA((STEPS, 13)), pltpu.SemaphoreType.DMA((STEPS, 13)),
    ]
    state = pl.pallas_call(
        functools.partial(kernel, n_lon, n_lat, lev),
        out_shape=jax.ShapeDtypeStruct((4, cells, cols), F32),
        in_specs=[hbm] * 10,
        out_specs=vmem,
        scratch_shapes=scratch,
        compiler_params=pltpu.CompilerParams(
            collective_id=0, has_side_effects=True, vmem_limit_bytes=56 * 1024 * 1024
        ),
        name="adjoint",
    )(*flat, flags, sea_mask.reshape(cells, cols), block_inverse, coupling)
    grads = pl.pallas_call(
        store,
        out_shape=[jax.ShapeDtypeStruct((cells, cols), F32)] * 4,
        in_specs=[anywhere],
        out_specs=[hbm] * 4,
        scratch_shapes=[pltpu.SemaphoreType.DMA((4,))],
        compiler_params=pltpu.CompilerParams(vmem_limit_bytes=8 * 1024 * 1024),
        name="store",
    )(state)
    return tuple(g.reshape(lev, rows, cols) for g in grads)


def solution(mesh):
    field = P("depth", "lat", "lon")
    in_specs = (field,) * 6 + (P(None, "depth", "lat", "lon"), field, P("lat", "depth", None), P("lat"))
    return jax.shard_map(
        functools.partial(on_device, mesh.shape["lon"], mesh.shape["lat"]),
        mesh=mesh,
        in_specs=in_specs,
        out_specs=(field,) * 4,
        check_vma=False,
    )
```

```python
import functools

import jax
import jax.numpy as jnp
from jax import lax
from jax.experimental import pallas as pl
from jax.experimental.pallas import tpu as pltpu
from jax.sharding import PartitionSpec as P

MESH = pl.DeviceIdType.MESH
F32, BF16, I32 = jnp.float32, jnp.bfloat16, jnp.int32

STEPS = 2
advect_scale = 0.25
diffusion = 0.5
gravity = 0.1
pressure_scale = 1.0
viscosity = 0.1
haline = 0.8

CORNER, PLANE, ZU, ZV, ZS = 0, 1, 5, 6, 7
LOW, HIGH = 0, 1
DEP, LON, LAT, DLON, DLAT, COEF, MISC = 0, 1, 3, 5, 7, 9, 11


def tile(k):
    return pl.ds(pl.multiple_of(k * 8, 8), 8)


def split(value):
    high = value.astype(BF16)
    return high, (value - high.astype(F32)).astype(BF16)


def kernel(
    n_lon, n_lat, lev,
    a_t, a_s, a_u, a_v, es_h, ns_h, fl_h, sea_h, inv_h, coup_h,
    out,
    st, es, ns, fl, sea_i, inv,
    sea, cs, sh, e_own, w_own, n_own, s_own, c0, proj, hx, enh, w3,
    wlat, cs_lat, spike, q, pc,
    d_s, d_r, lon_s, lon_r, lat_s, lat_r, coef_s, coef_r, misc_s, misc_r, dl_s, dl_r, dt_s, dt_r,
    coup, in_sem, send_sem, recv_sem,
):
    lon, lat, dep = lax.axis_index("lon"), lax.axis_index("lat"), lax.axis_index("depth")
    edge = (lev - 1) * (1 - dep)
    cells = lev * 8
    east, west = lax.rem(lon + 1, n_lon), lax.rem(lon + n_lon - 1, n_lon)
    has_low, has_high = lat > 0, lat < n_lat - 1
    other = 1 - dep

    barrier = pltpu.get_barrier_semaphore()

    def greet(device):
        pl.semaphore_signal(barrier, inc=1, device_id=device, device_id_type=MESH)

    for depth in (other, dep):
        greet((east, lat, depth))
        greet((west, lat, depth))
        if depth is other:
            greet((lon, lat, other))

        @pl.when(has_low)
        def _():
            greet((lon, lat - 1, depth))

        @pl.when(has_high)
        def _():
            greet((lon, lat + 1, depth))

    loads = []
    for i, (src, dst) in enumerate(
        [(inv_h, inv), (a_t, st.at[0]), (a_s, st.at[1]), (a_u, st.at[2]), (a_v, st.at[3]),
         (sea_h, sea_i), (es_h, es), (ns_h, ns), (fl_h, fl), (coup_h, coup)]
    ):
        copy = pltpu.make_async_copy(src, dst, in_sem.at[i])
        copy.start()
        loads.append(copy)

    lane = lax.broadcasted_iota(I32, (8, 128), 1)
    sub = lax.broadcasted_iota(I32, (8, 128), 0)
    first_lane, last_lane = lane == 0, lane == 127
    first_sub, last_sub = sub == 0, sub == 7
    zero = jnp.zeros((8, 128), F32)

    def to_east(a, halo):
        return jnp.where(last_lane, halo, pltpu.roll(a, 127, 1))

    def to_west(a, halo):
        return jnp.where(first_lane, halo, pltpu.roll(a, 1, 1))

    def to_north(a, halo):
        return jnp.where(last_sub, halo, pltpu.roll(a, 7, 0))

    def to_south(a, halo):
        return jnp.where(first_sub, halo, pltpu.roll(a, 1, 0))

    def copies(step):
        def remote(slot, src, dst, device):
            return pltpu.make_async_remote_copy(
                src_ref=src, dst_ref=dst, send_sem=send_sem.at[step, slot],
                recv_sem=recv_sem.at[step, slot], device_id=device, device_id_type=MESH,
            )

        first = step == 0
        upward = pl.ds(0, 8) if first else pl.ds(1, 6)
        downward = pl.ds(0, 5) if first else pl.ds(1, 4)
        todo = {}
        todo["up"] = (remote(DEP, d_s.at[step, upward], d_r.at[step, upward], (lon, lat, other)), dep == 1, dep == 0)
        todo["down"] = (remote(DEP, d_s.at[step, downward], d_r.at[step, downward], (lon, lat, other)), dep == 0, dep == 1)
        for side in (LOW, HIGH):
            far = 1 - side
            beside = east if side == HIGH else west
            row = lat + 1 if side == HIGH else lat - 1
            sends, gets = (has_high, has_low) if side == HIGH else (has_low, has_high)
            todo["dlon", side] = (remote(DLON + side, dl_s.at[step, side], dl_r.at[step, far], (beside, lat, other)), None, None)
            todo["dlat", side] = (remote(DLAT + side, dt_s.at[step, side], dt_r.at[step, far], (lon, row, other)), sends, gets)
            todo["lon", side] = (remote(LON + side, lon_s.at[step, side], lon_r.at[step, far], (beside, lat, dep)), None, None)
            todo["lat", side] = (remote(LAT + side, lat_s.at[step, side], lat_r.at[step, far], (lon, row, dep)), sends, gets)
            if first:
                count = 3 if side == HIGH else 1
                todo["coef", side] = (
                    remote(COEF + side, coef_s.at[side, pl.ds(0, count)], coef_r.at[far, pl.ds(0, count)], (lon, row, dep)), sends, gets)
                todo["misc", side] = (remote(MISC + side, misc_s, misc_r.at[far], (lon, row, dep)), sends, gets)
        return todo

    def act(entry, what):
        descriptor, sends, gets = entry
        call = {"start": descriptor.start, "send": descriptor.wait_send, "recv": descriptor.wait_recv}[what]
        condition = gets if what == "recv" else sends
        if condition is None:
            call()
        else:
            pl.when(condition)(call)

    for side, missing in ((LOW, lat == 0), (HIGH, lat == n_lat - 1)):

        @pl.when(missing)
        def _():
            for step in range(STEPS):
                lat_r[step, side] = jnp.zeros(lat_r.shape[2:], F32)
                dt_r[step, side] = zero
            coef_r[side] = jnp.zeros(coef_r.shape[1:], F32)
            misc_r[side] = jnp.zeros(misc_r.shape[1:], F32)

    loads[0].wait()
    loads[9].wait()
    coupling = zero
    for y in range(8):
        coupling = jnp.where(sub == y, coup[y], coupling)
    spike[...] = zero
    for y in range(8):
        spike[y : y + 1, 0:lev] = inv[y, pl.ds(edge, 1), :]
        high, low = split(inv[y])
        w3[y] = jnp.concatenate([high, high, low], axis=0)
        at_edge = lax.broadcasted_iota(I32, (lev, lev), 1) == edge
        column = jnp.sum(jnp.where(at_edge, inv[y], 0.0), axis=1, keepdims=True)
        pc[pl.ds(y, lev, stride=8), :] = jnp.broadcast_to(column, (lev, 128))
    spike_rows = spike[...]
    corner = jnp.broadcast_to(
        jnp.sum(jnp.where(lane == edge, spike_rows, 0.0), axis=1, keepdims=True), (8, 128)
    )
    scaled = spike_rows * coupling
    for k in range(lev):
        cs[tile(k)] = jnp.broadcast_to(scaled[:, k : k + 1], (8, 128))
    misc_s[0] = scaled
    misc_s[1] = coupling
    misc_s[2] = corner

    def project(step):
        for y in range(8):
            rows = pl.ds(y, lev, stride=8)
            column = jnp.concatenate([st[f, rows, :] for f in range(4)], axis=1)
            high, low = split(column)
            stacked = jnp.concatenate([high, low, high], axis=0)
            result = lax.dot_general(
                w3[y], stacked, (((0,), (0,)), ((), ())), preferred_element_type=F32
            )
            for f in range(4):
                part = result[:, f * 128 : (f + 1) * 128]
                proj[f, rows, :] = part
                if y == 0:
                    lat_s[step, LOW, f] = part
                if y == 7:
                    lat_s[step, HIGH, f] = part

    for copy in loads[1:5]:
        copy.wait()
    project(0)

    for copy in loads[5:9]:
        copy.wait()

    def prepare(k, carry):
        t = tile(k)
        mask = sea_i[t].astype(F32)
        sea[t] = mask
        quarter = mask * advect_scale
        speed_e, speed_n = es[t], ns[t]
        for n in range(STEPS):
            flag = fl[n, t]
            third = lax.shift_right_logical(flag * 11, 5)
            zonal = (flag - 3 * third).astype(F32) * 0.5
            merid = third.astype(F32) * 0.5
            e_own[n, t] = quarter * (speed_e * (1.0 - zonal) + diffusion)
            w_own[n, t] = quarter * (speed_e * zonal - diffusion)
            n_own[n, t] = quarter * (speed_n * (1.0 - merid) + diffusion)
            s_own[n, t] = quarter * (speed_n * merid - diffusion)
        return carry + mask * cs[t]

    spike_sum = lax.fori_loop(0, lev, prepare, zero, unroll=4)
    d_s[0, CORNER] = corner
    d_s[0, ZS] = spike_sum
    for side, y in ((LOW, 0), (HIGH, 7)):
        rows = pl.ds(y, lev, stride=8)
        coef_s[side, 0] = sea[rows, :]
        if side == HIGH:
            for n in range(STEPS):
                coef_s[side, 1 + n] = s_own[n, rows, :]

    for y in range(8):
        rows = pl.ds(y, lev, stride=8)
        ones = sea[rows, :].astype(BF16)
        high, low = split(inv[y])
        q[rows, :] = jnp.dot(high, ones, preferred_element_type=F32) + jnp.dot(low, ones, preferred_element_type=F32)

    pick_row = lax.broadcasted_iota(I32, (16, 128), 0)
    pick_lane = lax.broadcasted_iota(I32, (16, 128), 1)
    pick_edge = pick_lane == jnp.where(pick_row < 8, 0, 127)

    def first_sums():
        def sums(k, carry):
            t = tile(k)
            return carry[0] + sea[t] * proj[2, t], carry[1] + sea[t] * proj[3, t]

        both = lax.fori_loop(0, lev, sums, (zero, zero), unroll=8)
        return [proj[f, tile(edge)] for f in range(4)] + list(both)

    def messages(step, sent):
        planes, z_u, z_v = list(sent[:4]), sent[4], sent[5]
        for f in range(4):
            d_s[step, PLANE + f] = planes[f]
        d_s[step, ZU] = z_u
        d_s[step, ZV] = z_v
        for side, x in ((LOW, 0), (HIGH, 127)):
            packed = zero
            for i, value in enumerate(planes + [z_u, spike_sum]):
                packed = jnp.where(lane == i, jnp.broadcast_to(value[:, x : x + 1], (8, 128)), packed)
            dl_s[step, side] = packed
        for side, y in ((LOW, 0), (HIGH, 7)):
            for i, value in enumerate([corner] + planes + [z_v, spike_sum]):
                dt_s[step, side, i : i + 1, :] = value[y : y + 1, :]
            dt_s[step, side, 7:8, :] = zero[0:1, :]

    def edges(step):
        fields = [proj.at[f] for f in range(4)]
        if step == 0:
            fields = fields + [sea, w_own.at[0], w_own.at[1]]
        total = jnp.zeros((16, cells), F32)
        for i, field in enumerate(fields):
            pick = jnp.where(pick_edge & (lax.rem(pick_row, 8) == i), 1.0, 0.0).astype(BF16)
            for part in split(field[...]):
                total += lax.dot_general(
                    pick, part, (((1,), (1,)), ((), ())), preferred_element_type=F32
                )
        lon_s[step, LOW] = total[0:8]
        lon_s[step, HIGH] = total[8:16]

    def spread(step):
        count = 7 if step == 0 else 4
        parts = []
        for side in (HIGH, LOW):
            value = lon_r[step, side]
            high = value.astype(BF16).astype(F32)
            parts += [high, value - high]
        stacked = jnp.concatenate(parts, axis=0).astype(BF16)
        row = lax.broadcasted_iota(I32, (32, 128), 0)
        at = lax.broadcasted_iota(I32, (32, 128), 1) == jnp.where(row < 16, 127, 0)
        place = jnp.concatenate(
            [jnp.where(at & (lax.rem(row, 8) == i), 1.0, 0.0) for i in range(count)], axis=1
        ).astype(BF16)
        wide = lax.dot_general(stacked, place, (((0,), (0,)), ((), ())), preferred_element_type=F32)
        for i, field in enumerate([hx.at[0], hx.at[1], hx.at[2], hx.at[3], sh, enh.at[0], enh.at[1]][:count]):
            field[...] = wide[:, i * 128 : (i + 1) * 128]

    def faces(k, carry):
        t = tile(k)
        mask, halo = sea[t], sh[t]
        row = pl.ds(k, 1)
        mask_e = to_east(mask, halo)
        mask_n = to_north(mask, coef_r[HIGH, 0, row, :])
        for n in range(STEPS):
            e = e_own[n, t] * mask_e
            w = mask * to_west(w_own[n, t], enh[n, t])
            north = n_own[n, t] * mask_n
            south = mask * to_south(s_own[n, t], coef_r[LOW, 1 + n, row, :])
            e_own[n, t] = e
            w_own[n, t] = w
            n_own[n, t] = north
            s_own[n, t] = south
            c0[n, t] = (1.0 - e + w) - (north - south)
        return carry

    def spread_spikes():
        k_at = lax.broadcasted_iota(I32, (lev, 128), 0)
        same = k_at == lax.broadcasted_iota(I32, (lev, 128), 1)
        for side, y in ((LOW, 7), (HIGH, 0)):
            row = misc_r[side, 0, y : y + 1, :]
            column = jnp.sum(jnp.where(same, jnp.broadcast_to(row, (lev, 128)), 0.0), axis=1, keepdims=True)
            cs_lat[side] = jnp.broadcast_to(column, (lev, 128))

    row_at = (sub + lat * 8).astype(F32)
    coriolis = 0.2 + 0.6 * (row_at + 0.5) / (8.0 * n_lat)

    def advance(step, n, target):
        other_corner = d_r[0, CORNER]
        alpha = 1.0 / (1.0 - coupling * coupling * corner * other_corner)
        beta = coupling * other_corner * alpha
        gamma = coupling * corner * alpha
        own = [proj[f, tile(edge)] for f in range(4)]
        far = [d_r[step, PLANE + f] for f in range(4)]
        carried = [alpha * far[f] + beta * own[f] for f in range(4)]

        def beside(i):
            low = jnp.broadcast_to(dl_r[step, LOW, :, i : i + 1], (8, 128))
            high = jnp.broadcast_to(dl_r[step, HIGH, :, i : i + 1], (8, 128))
            return jnp.where(last_lane, high, jnp.where(first_lane, low, 0.0))

        own_side = [hx[f, tile(edge)] for f in range(4)]
        far_side = [beside(f) for f in range(4)]
        carried_side = [alpha * far_side[f] + beta * own_side[f] for f in range(4)]

        z_u = d_r[step, ZU] + d_r[0, ZS] * (alpha * own[2] + gamma * far[2])
        z_v = d_r[step, ZV] + d_r[0, ZS] * (alpha * own[3] + gamma * far[3])
        z_side = beside(4) + beside(5) * (alpha * own_side[2] + gamma * far_side[2])
        z_rows = []
        for side, y in ((LOW, 7), (HIGH, 0)):
            c = misc_r[side, 1, y : y + 1, :]
            mine = misc_r[side, 2, y : y + 1, :]
            theirs = dt_r[step, side, 0:1, :]
            a = 1.0 / (1.0 - c * c * mine * theirs)
            b = c * theirs * a
            g = c * mine * a
            mask = coef_r[side, 0]
            for f in range(4):
                near = lat_r[step, side, f, pl.ds(edge, 1), :]
                row = dt_r[step, side, 1 + f : 2 + f, :]
                carried_row = a * row + b * near
                wlat[side, f] = mask * (lat_r[step, side, f] + cs_lat[side] * carried_row)
                if f == 3:
                    z_rows.append(dt_r[step, side, 5:6, :] + dt_r[step, side, 6:7, :] * (a * near + g * row))
        deeper = -0.5 * pressure_scale * (
            to_west(z_u, z_side) - to_east(z_u, z_side)
            + to_south(z_v, z_rows[LOW]) - to_north(z_v, z_rows[HIGH])
        )
        deeper = jnp.where(dep == 0, deeper, 0.0)

        def level(i, carry):
            below, sent = carry[0], list(carry[1:])
            k = lev - 1 - i
            t = tile(k)
            row = pl.ds(k, 1)
            mask, tip, halo = sea[t], cs[t], sh[t]
            w, e_, w_, n_, s_ = [], [], [], [], []
            for f in range(4):
                here = mask * (proj[f, t] + tip * carried[f])
                side = halo * (hx[f, t] + tip * carried_side[f])
                w.append(here)
                e_.append(to_east(here, side))
                w_.append(to_west(here, side))
                n_.append(to_north(here, wlat[HIGH, f, row, :]))
                s_.append(to_south(here, wlat[LOW, f, row, :]))
            below = below + (-0.5 * pressure_scale) * (w_[2] - e_[2] + s_[3] - n_[3])
            lift = gravity * below
            ce, cw, cn, cs_, cc = e_own[n, t], w_own[n, t], n_own[n, t], s_own[n, t], c0[n, t]
            new = [
                (cc * w[f] + ce * e_[f]) + (cn * n_[f] - cw * w_[f]) + (part - cs_ * s_[f])
                for f, part in ((0, lift), (1, -haline * lift))
            ]
            for f, turn in ((2, -coriolis * w[3]), (3, coriolis * w[2])):
                around = (e_[f] + w_[f]) + (n_[f] + s_[f])
                new.append((1.0 - 4.0 * viscosity) * w[f] + turn + viscosity * around)
            for f in range(4):
                target[f, t] = new[f]
            if sent:
                weight, mass = pc[t], q[t]
                for f in range(4):
                    sent[f] = sent[f] + weight * new[f]
                sent[4] = sent[4] + mass * new[2]
                sent[5] = sent[5] + mass * new[3]
            return (below, *sent)

        following = (zero,) * 6 if step < STEPS - 1 else ()
        return lax.fori_loop(0, lev, level, (deeper, *following), unroll=8)[1:]

    messages(0, first_sums())
    edges(0)
    todo = [copies(0), copies(1)]
    pl.semaphore_wait(barrier, 5 + 2 * has_low.astype(I32) + 2 * has_high.astype(I32))

    for step in range(STEPS):
        now = todo[step]
        if step > 0:
            messages(step, sent)
        order = [("dlon", side) for side in (LOW, HIGH)] + ["up", "down"] + [("dlat", side) for side in (LOW, HIGH)]
        for name in order:
            act(now[name], "start")
        if step > 0:
            project(step)
            edges(step)
        rest = [(kind, side) for kind in ("lon", "misc", "coef", "lat") for side in (LOW, HIGH)]
        for name in rest:
            if name in now:
                act(now[name], "start")
        for name in rest:
            if name in now:
                act(now[name], "recv")
        spread(step)
        if step == 0:
            spread_spikes()
            lax.fori_loop(0, lev, faces, 0, unroll=4)
        for name in order:
            act(now[name], "recv")
        sent = advance(step, STEPS - 1 - step, st if step < STEPS - 1 else out)
    for now in todo:
        for entry in now.values():
            act(entry, "send")


def store(state, *rest):
    outs, sem = rest[:4], rest[4]
    moves = [pltpu.make_async_copy(state.at[f], outs[f], sem.at[f]) for f in range(4)]
    for move in moves:
        move.start()
    for move in moves:
        move.wait()


def on_device(
    n_lon, n_lat,
    adj_temp, adj_salt, adj_zonal, adj_merid, east_speed, north_speed, branch_flags, sea_mask, block_inverse, coupling,
):
    lev, rows, cols = adj_temp.shape
    cells = lev * rows
    flat = [v.reshape(cells, cols) for v in (adj_temp, adj_salt, adj_zonal, adj_merid, east_speed, north_speed)]
    flags = branch_flags.reshape(STEPS, cells, cols)
    hbm = pl.BlockSpec(memory_space=pltpu.HBM)
    anywhere = pl.BlockSpec(memory_space=pl.ANY)
    vmem = pl.BlockSpec(memory_space=pltpu.VMEM)
    field = pltpu.VMEM((cells, cols), F32)

    def fields(*lead):
        return pltpu.VMEM((*lead, cells, cols), F32)

    def tiles(*lead):
        return pltpu.VMEM((*lead, 8, 128), F32)

    scratch = [
        fields(4), field, field, pltpu.VMEM((STEPS, cells, cols), I32), pltpu.VMEM((cells, cols), I32),
        pltpu.VMEM((rows, lev, lev), F32),
        field, field, field,
        fields(STEPS), fields(STEPS), fields(STEPS), fields(STEPS), fields(STEPS),
        fields(4), fields(4), fields(STEPS), pltpu.VMEM((rows, 3 * lev, lev), BF16),
        pltpu.VMEM((2, 4, lev, 128), F32), pltpu.VMEM((2, lev, 128), F32), tiles(), field, field,
        tiles(STEPS, 8), tiles(STEPS, 8),
        pltpu.VMEM((STEPS, 2, 8, cells), F32), pltpu.VMEM((STEPS, 2, 8, cells), F32),
        pltpu.VMEM((STEPS, 2, 4, lev, 128), F32), pltpu.VMEM((STEPS, 2, 4, lev, 128), F32),
        pltpu.VMEM((2, 3, lev, 128), F32), pltpu.VMEM((2, 3, lev, 128), F32),
        tiles(3), tiles(2, 3),
        tiles(STEPS, 2), tiles(STEPS, 2), tiles(STEPS, 2), tiles(STEPS, 2),
        pltpu.SMEM((rows,), F32), pltpu.SemaphoreType.DMA((10,)),
        pltpu.SemaphoreType.DMA((STEPS, 13)), pltpu.SemaphoreType.DMA((STEPS, 13)),
    ]
    state = pl.pallas_call(
        functools.partial(kernel, n_lon, n_lat, lev),
        out_shape=jax.ShapeDtypeStruct((4, cells, cols), F32),
        in_specs=[hbm] * 10,
        out_specs=vmem,
        scratch_shapes=scratch,
        compiler_params=pltpu.CompilerParams(
            collective_id=0, has_side_effects=True, vmem_limit_bytes=40 * 1024 * 1024
        ),
        name="adjoint",
    )(*[pltpu.with_memory_space_constraint(v, pltpu.HBM) for v in (*flat, flags, sea_mask.reshape(cells, cols), block_inverse, coupling)])
    grads = pl.pallas_call(
        store,
        out_shape=[jax.ShapeDtypeStruct((cells, cols), F32)] * 4,
        in_specs=[anywhere],
        out_specs=[hbm] * 4,
        scratch_shapes=[pltpu.SemaphoreType.DMA((4,))],
        compiler_params=pltpu.CompilerParams(vmem_limit_bytes=8 * 1024 * 1024),
        name="store",
    )(state)
    return tuple(g.reshape(lev, rows, cols) for g in grads)


def solution(mesh):
    field = P("depth", "lat", "lon")
    in_specs = (field,) * 6 + (P(None, "depth", "lat", "lon"), field, P("lat", "depth", None), P("lat"))
    return jax.shard_map(
        functools.partial(on_device, mesh.shape["lon"], mesh.shape["lat"]),
        mesh=mesh,
        in_specs=in_specs,
        out_specs=(field,) * 4,
        check_vma=False,
    )
```

```python
import functools

import jax
import jax.numpy as jnp
from jax import lax
from jax.experimental import pallas as pl
from jax.experimental.pallas import tpu as pltpu
from jax.sharding import PartitionSpec as P

MESH = pl.DeviceIdType.MESH
F32, BF16, I32 = jnp.float32, jnp.bfloat16, jnp.int32

STEPS = 2
advect_scale = 0.25
diffusion = 0.5
gravity = 0.1
pressure_scale = 1.0
viscosity = 0.1
haline = 0.8

CORNER, PLANE, ZU, ZV, ZS = 0, 1, 5, 6, 7
LOW, HIGH = 0, 1
DEP, LON, LAT, DLON, DLAT, COEF, MISC = 0, 1, 3, 5, 7, 9, 11


def tile(k):
    return pl.ds(pl.multiple_of(k * 8, 8), 8)


def split(value):
    high = value.astype(BF16)
    return high, (value - high.astype(F32)).astype(BF16)


def kernel(
    n_lon, n_lat, lev,
    a_t, a_s, a_u, a_v, es_h, ns_h, fl_h, sea_h, inv_h, coup_h,
    out,
    st, es, ns, fl, sea_i, inv,
    sea, cs, sh, e_own, w_own, n_own, s_own, c0, proj, hx, enh, w3,
    wlat, cs_lat, spike, q, pc, m5,
    d_s, d_r, lon_s, lon_r, lat_s, lat_r, coef_s, coef_r, misc_s, misc_r, dl_s, dl_r, dt_s, dt_r,
    coup, in_sem, send_sem, recv_sem,
):
    lon, lat, dep = lax.axis_index("lon"), lax.axis_index("lat"), lax.axis_index("depth")
    edge = (lev - 1) * (1 - dep)
    cells = lev * 8
    east, west = lax.rem(lon + 1, n_lon), lax.rem(lon + n_lon - 1, n_lon)
    has_low, has_high = lat > 0, lat < n_lat - 1
    other = 1 - dep

    barrier = pltpu.get_barrier_semaphore()

    def greet(device):
        pl.semaphore_signal(barrier, inc=1, device_id=device, device_id_type=MESH)

    for depth in (other, dep):
        greet((east, lat, depth))
        greet((west, lat, depth))
        if depth is other:
            greet((lon, lat, other))

        @pl.when(has_low)
        def _():
            greet((lon, lat - 1, depth))

        @pl.when(has_high)
        def _():
            greet((lon, lat + 1, depth))

    loads = []
    for i, (src, dst) in enumerate(
        [(inv_h, inv), (a_t, st.at[0]), (a_s, st.at[1]), (a_u, st.at[2]), (a_v, st.at[3]),
         (sea_h, sea_i), (es_h, es), (ns_h, ns), (fl_h, fl), (coup_h, coup)]
    ):
        copy = pltpu.make_async_copy(src, dst, in_sem.at[i])
        copy.start()
        loads.append(copy)

    lane = lax.broadcasted_iota(I32, (8, 128), 1)
    sub = lax.broadcasted_iota(I32, (8, 128), 0)
    first_lane, last_lane = lane == 0, lane == 127
    first_sub, last_sub = sub == 0, sub == 7
    zero = jnp.zeros((8, 128), F32)

    def to_east(a, halo):
        return jnp.where(last_lane, halo, pltpu.roll(a, 127, 1))

    def to_west(a, halo):
        return jnp.where(first_lane, halo, pltpu.roll(a, 1, 1))

    def to_north(a, halo):
        return jnp.where(last_sub, halo, pltpu.roll(a, 7, 0))

    def to_south(a, halo):
        return jnp.where(first_sub, halo, pltpu.roll(a, 1, 0))

    def copies(step):
        def remote(slot, src, dst, device):
            return pltpu.make_async_remote_copy(
                src_ref=src, dst_ref=dst, send_sem=send_sem.at[step, slot],
                recv_sem=recv_sem.at[step, slot], device_id=device, device_id_type=MESH,
            )

        first = step == 0
        upward = pl.ds(0, 8) if first else pl.ds(1, 6)
        downward = pl.ds(0, 5) if first else pl.ds(1, 4)
        todo = {}
        todo["up"] = (remote(DEP, d_s.at[step, upward], d_r.at[step, upward], (lon, lat, other)), dep == 1, dep == 0)
        todo["down"] = (remote(DEP, d_s.at[step, downward], d_r.at[step, downward], (lon, lat, other)), dep == 0, dep == 1)
        for side in (LOW, HIGH):
            far = 1 - side
            beside = east if side == HIGH else west
            row = lat + 1 if side == HIGH else lat - 1
            sends, gets = (has_high, has_low) if side == HIGH else (has_low, has_high)
            todo["dlon", side] = (remote(DLON + side, dl_s.at[step, side], dl_r.at[step, far], (beside, lat, other)), None, None)
            todo["dlat", side] = (remote(DLAT + side, dt_s.at[step, side], dt_r.at[step, far], (lon, row, other)), sends, gets)
            todo["lon", side] = (remote(LON + side, lon_s.at[step, side], lon_r.at[step, far], (beside, lat, dep)), None, None)
            todo["lat", side] = (remote(LAT + side, lat_s.at[step, side], lat_r.at[step, far], (lon, row, dep)), sends, gets)
            if first:
                count = 3 if side == HIGH else 1
                todo["coef", side] = (
                    remote(COEF + side, coef_s.at[side, pl.ds(0, count)], coef_r.at[far, pl.ds(0, count)], (lon, row, dep)), sends, gets)
                todo["misc", side] = (remote(MISC + side, misc_s, misc_r.at[far], (lon, row, dep)), sends, gets)
        return todo

    def act(entry, what):
        descriptor, sends, gets = entry
        call = {"start": descriptor.start, "send": descriptor.wait_send, "recv": descriptor.wait_recv}[what]
        condition = gets if what == "recv" else sends
        if condition is None:
            call()
        else:
            pl.when(condition)(call)

    for side, missing in ((LOW, lat == 0), (HIGH, lat == n_lat - 1)):

        @pl.when(missing)
        def _():
            for step in range(STEPS):
                lat_r[step, side] = jnp.zeros(lat_r.shape[2:], F32)
                dt_r[step, side] = zero
            coef_r[side] = jnp.zeros(coef_r.shape[1:], F32)
            misc_r[side] = jnp.zeros(misc_r.shape[1:], F32)

    loads[0].wait()
    loads[9].wait()
    coupling = zero
    for y in range(8):
        coupling = jnp.where(sub == y, coup[y], coupling)
    spike[...] = zero
    for y in range(8):
        spike[y : y + 1, 0:lev] = inv[y, pl.ds(edge, 1), :]
        high, low = split(inv[y])
        w3[y] = jnp.concatenate([high, high, low], axis=0)
        at_edge = lax.broadcasted_iota(I32, (lev, lev), 1) == edge
        column = jnp.sum(jnp.where(at_edge, inv[y], 0.0), axis=1, keepdims=True)
        pc[pl.ds(y, lev, stride=8), :] = jnp.broadcast_to(column, (lev, 128))
    spike_rows = spike[...]
    corner = jnp.broadcast_to(
        jnp.sum(jnp.where(lane == edge, spike_rows, 0.0), axis=1, keepdims=True), (8, 128)
    )
    scaled = spike_rows * coupling
    for k in range(lev):
        cs[tile(k)] = jnp.broadcast_to(scaled[:, k : k + 1], (8, 128))
    misc_s[0] = scaled
    misc_s[1] = coupling
    misc_s[2] = corner

    def project(step):
        for y in range(8):
            rows = pl.ds(y, lev, stride=8)
            column = jnp.concatenate([st[f, rows, :] for f in range(4)], axis=1)
            high, low = split(column)
            stacked = jnp.concatenate([high, low, high], axis=0)
            result = lax.dot_general(
                w3[y], stacked, (((0,), (0,)), ((), ())), preferred_element_type=F32
            )
            for f in range(4):
                part = result[:, f * 128 : (f + 1) * 128]
                proj[f, rows, :] = part
                if y == 0:
                    lat_s[step, LOW, f] = part
                if y == 7:
                    lat_s[step, HIGH, f] = part

    for copy in loads[1:5]:
        copy.wait()
    project(0)

    for copy in loads[5:9]:
        copy.wait()

    def prepare(k, carry):
        t = tile(k)
        mask = sea_i[t].astype(F32)
        sea[t] = mask
        quarter = mask * advect_scale
        speed_e, speed_n = es[t], ns[t]
        for n in range(STEPS):
            flag = fl[n, t]
            third = lax.shift_right_logical(flag * 11, 5)
            zonal = (flag - 3 * third).astype(F32) * 0.5
            merid = third.astype(F32) * 0.5
            e_own[n, t] = quarter * (speed_e * (1.0 - zonal) + diffusion)
            w_own[n, t] = quarter * (speed_e * zonal - diffusion)
            n_own[n, t] = quarter * (speed_n * (1.0 - merid) + diffusion)
            s_own[n, t] = quarter * (speed_n * merid - diffusion)
        return carry[0] + mask * cs[t], carry[1] + pc[t]

    spike_sum, pc_sum = lax.fori_loop(0, lev, prepare, (zero, zero), unroll=4)
    d_s[0, CORNER] = corner
    d_s[0, ZS] = spike_sum
    for side, y in ((LOW, 0), (HIGH, 7)):
        rows = pl.ds(y, lev, stride=8)
        coef_s[side, 0] = sea[rows, :]
        if side == HIGH:
            for n in range(STEPS):
                coef_s[side, 1 + n] = s_own[n, rows, :]

    for y in range(8):
        rows = pl.ds(y, lev, stride=8)
        ones = sea[rows, :].astype(BF16)
        high, low = split(inv[y])
        q[rows, :] = jnp.dot(high, ones, preferred_element_type=F32) + jnp.dot(low, ones, preferred_element_type=F32)

    pick_row = lax.broadcasted_iota(I32, (16, 128), 0)
    pick_lane = lax.broadcasted_iota(I32, (16, 128), 1)
    pick_edge = pick_lane == jnp.where(pick_row < 8, 0, 127)

    def first_sums():
        def sums(k, carry):
            t = tile(k)
            return carry[0] + sea[t] * proj[2, t], carry[1] + sea[t] * proj[3, t]

        both = lax.fori_loop(0, lev, sums, (zero, zero), unroll=8)
        return [proj[f, tile(edge)] for f in range(4)] + list(both)

    def messages(step, sent):
        planes, z_u, z_v = list(sent[:4]), sent[4], sent[5]
        for f in range(4):
            d_s[step, PLANE + f] = planes[f]
        d_s[step, ZU] = z_u
        d_s[step, ZV] = z_v
        for side, x in ((LOW, 0), (HIGH, 127)):
            packed = zero
            for i, value in enumerate(planes + [z_u, spike_sum]):
                packed = jnp.where(lane == i, jnp.broadcast_to(value[:, x : x + 1], (8, 128)), packed)
            dl_s[step, side] = packed
        for side, y in ((LOW, 0), (HIGH, 7)):
            for i, value in enumerate([corner] + planes + [z_v, spike_sum]):
                dt_s[step, side, i : i + 1, :] = value[y : y + 1, :]
            dt_s[step, side, 7:8, :] = zero[0:1, :]

    def edges(step):
        fields = [proj.at[f] for f in range(4)]
        if step == 0:
            fields = fields + [sea, w_own.at[0], w_own.at[1]]
        total = jnp.zeros((16, cells), F32)
        for i, field in enumerate(fields):
            pick = jnp.where(pick_edge & (lax.rem(pick_row, 8) == i), 1.0, 0.0).astype(BF16)
            for part in split(field[...]):
                total += lax.dot_general(
                    pick, part, (((1,), (1,)), ((), ())), preferred_element_type=F32
                )
        lon_s[step, LOW] = total[0:8]
        lon_s[step, HIGH] = total[8:16]

    def spread(step):
        count = 7 if step == 0 else 4
        parts = []
        for side in (HIGH, LOW):
            value = lon_r[step, side]
            high = value.astype(BF16).astype(F32)
            parts += [high, value - high]
        stacked = jnp.concatenate(parts, axis=0).astype(BF16)
        row = lax.broadcasted_iota(I32, (32, 128), 0)
        at = lax.broadcasted_iota(I32, (32, 128), 1) == jnp.where(row < 16, 127, 0)
        place = jnp.concatenate(
            [jnp.where(at & (lax.rem(row, 8) == i), 1.0, 0.0) for i in range(count)], axis=1
        ).astype(BF16)
        wide = lax.dot_general(stacked, place, (((0,), (0,)), ((), ())), preferred_element_type=F32)
        for i, field in enumerate([hx.at[0], hx.at[1], hx.at[2], hx.at[3], sh, enh.at[0], enh.at[1]][:count]):
            field[...] = wide[:, i * 128 : (i + 1) * 128]

    def faces(n, k, carry):
        t = tile(k)
        mask, halo = sea[t], sh[t]
        row = pl.ds(k, 1)
        mask_e = to_east(mask, halo)
        mask_n = to_north(mask, coef_r[HIGH, 0, row, :])
        e = e_own[n, t] * mask_e
        w = mask * to_west(w_own[n, t], enh[n, t])
        north = n_own[n, t] * mask_n
        south = mask * to_south(s_own[n, t], coef_r[LOW, 1 + n, row, :])
        e_own[n, t] = e
        w_own[n, t] = w
        n_own[n, t] = north
        s_own[n, t] = south
        c0[n, t] = (1.0 - e + w) - (north - south)
        return carry

    def spread_spikes():
        k_at = lax.broadcasted_iota(I32, (lev, 128), 0)
        same = k_at == lax.broadcasted_iota(I32, (lev, 128), 1)
        for side, y in ((LOW, 7), (HIGH, 0)):
            row = misc_r[side, 0, y : y + 1, :]
            column = jnp.sum(jnp.where(same, jnp.broadcast_to(row, (lev, 128)), 0.0), axis=1, keepdims=True)
            cs_lat[side] = jnp.broadcast_to(column, (lev, 128))

    row_at = (sub + lat * 8).astype(F32)
    coriolis = 0.2 + 0.6 * (row_at + 0.5) / (8.0 * n_lat)

    def masses():
        def level(i, carry):
            k = lev - 1 - i
            t = tile(k)
            row = pl.ds(k, 1)
            here = sea[t] * cs[t]
            side = sh[t] * cs[t]
            values = [
                here, to_east(here, side), to_west(here, side),
                to_north(here, coef_r[HIGH, 0, row, :] * cs_lat[HIGH, row, :]),
                to_south(here, coef_r[LOW, 0, row, :] * cs_lat[LOW, row, :]),
            ]
            for j in range(5):
                m5[j, t] = values[j]
            above, by_plane, by_above, by_mass = carry
            weight, mass = pc[t], q[t]
            return (
                above - weight,
                tuple(c + weight * v for c, v in zip(by_plane, values)),
                tuple(c + above * v for c, v in zip(by_above, values[1:])),
                tuple(c + mass * v for c, v in zip(by_mass, values)),
            )

        return lax.fori_loop(0, lev, level, (pc_sum, (zero,) * 5, (zero,) * 4, (zero,) * 5), unroll=8)[1:]

    half = 0.5 * pressure_scale

    def base(step, n, target):
        for side in (LOW, HIGH):
            for f in range(4):
                wlat[side, f] = coef_r[side, 0] * lat_r[step, side, f]
        count = 11 if step < STEPS - 1 else 0

        def level(i, carry):
            below, sums = carry[0], list(carry[1:])
            k = lev - 1 - i
            t = tile(k)
            row = pl.ds(k, 1)
            mask, halo = sea[t], sh[t]
            w, e_, w_, n_, s_ = [], [], [], [], []
            for f in range(4):
                here = mask * proj[f, t]
                side = halo * hx[f, t]
                w.append(here)
                e_.append(to_east(here, side))
                w_.append(to_west(here, side))
                n_.append(to_north(here, wlat[HIGH, f, row, :]))
                s_.append(to_south(here, wlat[LOW, f, row, :]))
            below = below + half * ((e_[2] - w_[2]) + (n_[3] - s_[3]))
            lift = gravity * below
            coefs = [c0[n, t], e_own[n, t], -w_own[n, t], n_own[n, t], -s_own[n, t]]
            new = [
                (coefs[0] * w[f] + coefs[1] * e_[f]) + (coefs[3] * n_[f] + coefs[2] * w_[f]) + (part + coefs[4] * s_[f])
                for f, part in ((0, lift), (1, -haline * lift))
            ]
            for f, turn in ((2, -coriolis * w[3]), (3, coriolis * w[2])):
                around = (e_[f] + w_[f]) + (n_[f] + s_[f])
                new.append((1.0 - 4.0 * viscosity) * w[f] + turn + viscosity * around)
            for f in range(4):
                target[f, t] = new[f]
            coefs = [c * m5[j, t] for j, c in enumerate(coefs)]
            for ref, c in zip((c0, e_own, w_own, n_own, s_own), coefs):
                ref[n, t] = c
            if sums:
                weight, mass = pc[t], q[t]
                for f in range(4):
                    sums[f] = sums[f] + weight * new[f]
                sums[4] = sums[4] + mass * new[2]
                sums[5] = sums[5] + mass * new[3]
                for j in range(5):
                    sums[6 + j] = sums[6 + j] + weight * coefs[j]
            return (below, *sums)

        return lax.fori_loop(0, lev, level, (zero,) * (1 + count), unroll=4)[1:]

    def carry_over(step):
        other_corner = d_r[0, CORNER]
        alpha = 1.0 / (1.0 - coupling * coupling * corner * other_corner)
        beta = coupling * other_corner * alpha
        gamma = coupling * corner * alpha
        own = [proj[f, tile(edge)] for f in range(4)]
        far = [d_r[step, PLANE + f] for f in range(4)]
        carried = [alpha * far[f] + beta * own[f] for f in range(4)]

        def beside(i):
            low = jnp.broadcast_to(dl_r[step, LOW, :, i : i + 1], (8, 128))
            high = jnp.broadcast_to(dl_r[step, HIGH, :, i : i + 1], (8, 128))
            return jnp.where(last_lane, high, jnp.where(first_lane, low, 0.0))

        own_side = [hx[f, tile(edge)] for f in range(4)]
        far_side = [beside(f) for f in range(4)]
        side = [alpha * far_side[f] + beta * own_side[f] for f in range(4)]

        z_u = d_r[step, ZU] + d_r[0, ZS] * (alpha * own[2] + gamma * far[2])
        z_v = d_r[step, ZV] + d_r[0, ZS] * (alpha * own[3] + gamma * far[3])
        z_side = beside(4) + beside(5) * (alpha * own_side[2] + gamma * far_side[2])
        z_rows, rows = [], []
        for at, y in ((LOW, 7), (HIGH, 0)):
            c = misc_r[at, 1, y : y + 1, :]
            mine = misc_r[at, 2, y : y + 1, :]
            theirs = dt_r[step, at, 0:1, :]
            a = 1.0 / (1.0 - c * c * mine * theirs)
            b = c * theirs * a
            g = c * mine * a
            near = [lat_r[step, at, f, pl.ds(edge, 1), :] for f in range(4)]
            row = [dt_r[step, at, 1 + f : 2 + f, :] for f in range(4)]
            rows.append([a * row[f] + b * near[f] for f in range(4)])
            z_rows.append(dt_r[step, at, 5:6, :] + dt_r[step, at, 6:7, :] * (a * near[3] + g * row[3]))
        deeper = half * (
            (to_east(z_u, z_side) - to_west(z_u, z_side))
            + (to_north(z_v, z_rows[HIGH]) - to_south(z_v, z_rows[LOW]))
        )
        deeper = jnp.where(dep == 0, deeper, 0.0)
        around = [
            (carried[f], to_east(carried[f], side[f]), to_west(carried[f], side[f]),
             to_north(carried[f], rows[HIGH][f]), to_south(carried[f], rows[LOW][f]))
            for f in range(4)
        ]
        turned = (
            (1.0 - 4.0 * viscosity) * carried[2] - coriolis * carried[3],
            (1.0 - 4.0 * viscosity) * carried[3] + coriolis * carried[2],
        )
        slow = [[viscosity * v for v in around[2 + f]] for f in range(2)]
        return around, turned, slow, deeper

    def combine(weights, values):
        terms = [a * b for a, b in zip(weights, values)]
        return (terms[0] + terms[1]) + (terms[2] + terms[3]) + sum(terms[4:], zero)

    def next_sums(sums, weights, interface):
        around, turned, slow, deeper = interface
        by_plane, by_above, by_mass = weights
        press = half * (by_above[0] * around[2][1] - by_above[1] * around[2][2] + by_above[2] * around[3][3] - by_above[3] * around[3][4])
        lift = gravity * (press + pc_sum * deeper)
        out_sums = [
            sums[f] + combine(sums[6:11], around[f]) + part for f, part in ((0, lift), (1, -haline * lift))
        ]
        for f in range(2):
            out_sums.append(sums[2 + f] + combine(by_plane, [turned[f]] + slow[f][1:]))
        for f in range(2):
            out_sums.append(sums[4 + f] + combine(by_mass, [turned[f]] + slow[f][1:]))
        return out_sums

    def finish(n, target, interface):
        around, turned, slow, deeper = interface

        def level(i, below):
            t = tile(lev - 1 - i)
            m = [m5[j, t] for j in range(5)]
            east_u, west_u = m[1] * around[2][1], m[2] * around[2][2]
            north_v, south_v = m[3] * around[3][3], m[4] * around[3][4]
            below = below + half * ((east_u - west_u) + (north_v - south_v))
            lift = gravity * below
            coefs = [c0[n, t], e_own[n, t], w_own[n, t], n_own[n, t], s_own[n, t]]
            target[0, t] = target[0, t] + combine(coefs, around[0]) + lift
            target[1, t] = target[1, t] + combine(coefs, around[1]) - haline * lift
            target[2, t] = (target[2, t] + m[0] * turned[0]) + viscosity * (east_u + west_u) + (m[3] * slow[0][3] + m[4] * slow[0][4])
            target[3, t] = (target[3, t] + m[0] * turned[1]) + viscosity * (north_v + south_v) + (m[1] * slow[1][1] + m[2] * slow[1][2])
            return below

        lax.fori_loop(0, lev, level, deeper, unroll=8)

    messages(0, first_sums())
    edges(0)
    todo = [copies(0), copies(1)]
    pl.semaphore_wait(barrier, 5 + 2 * has_low.astype(I32) + 2 * has_high.astype(I32))

    for step in range(STEPS):
        now = todo[step]
        order = [("dlon", side) for side in (LOW, HIGH)] + ["up", "down"] + [("dlat", side) for side in (LOW, HIGH)]
        if step == 0:
            for name in order:
                act(now[name], "start")
        else:
            project(step)
            edges(step)
        rest = [(kind, side) for kind in ("lon", "misc", "coef", "lat") for side in (LOW, HIGH)]
        for name in rest:
            if name in now:
                act(now[name], "start")
        if step > 0:
            lax.fori_loop(0, lev, functools.partial(faces, STEPS - 1 - step), 0, unroll=8)
        for name in rest:
            if name in now:
                act(now[name], "recv")
        spread(step)
        if step == 0:
            spread_spikes()
            lax.fori_loop(0, lev, functools.partial(faces, STEPS - 1), 0, unroll=8)
            weights = masses()
        n = STEPS - 1 - step
        target = st if step < STEPS - 1 else out
        sums = base(step, n, target)
        for name in order:
            act(now[name], "recv")
        interface = carry_over(step)
        if step < STEPS - 1:
            messages(step + 1, next_sums(sums, weights, interface))
            for name in order:
                act(todo[step + 1][name], "start")
        finish(n, target, interface)
    for now in todo:
        for entry in now.values():
            act(entry, "send")


def store(state, *rest):
    outs, sem = rest[:4], rest[4]
    moves = [pltpu.make_async_copy(state.at[f], outs[f], sem.at[f]) for f in range(4)]
    for move in moves:
        move.start()
    for move in moves:
        move.wait()


def on_device(
    n_lon, n_lat,
    adj_temp, adj_salt, adj_zonal, adj_merid, east_speed, north_speed, branch_flags, sea_mask, block_inverse, coupling,
):
    lev, rows, cols = adj_temp.shape
    cells = lev * rows
    flat = [v.reshape(cells, cols) for v in (adj_temp, adj_salt, adj_zonal, adj_merid, east_speed, north_speed)]
    flags = branch_flags.reshape(STEPS, cells, cols)
    hbm = pl.BlockSpec(memory_space=pltpu.HBM)
    anywhere = pl.BlockSpec(memory_space=pl.ANY)
    vmem = pl.BlockSpec(memory_space=pltpu.VMEM)
    field = pltpu.VMEM((cells, cols), F32)

    def fields(*lead):
        return pltpu.VMEM((*lead, cells, cols), F32)

    def tiles(*lead):
        return pltpu.VMEM((*lead, 8, 128), F32)

    scratch = [
        fields(4), field, field, pltpu.VMEM((STEPS, cells, cols), I32), pltpu.VMEM((cells, cols), I32),
        pltpu.VMEM((rows, lev, lev), F32),
        field, field, field,
        fields(STEPS), fields(STEPS), fields(STEPS), fields(STEPS), fields(STEPS),
        fields(4), fields(4), fields(STEPS), pltpu.VMEM((rows, 3 * lev, lev), BF16),
        pltpu.VMEM((2, 4, lev, 128), F32), pltpu.VMEM((2, lev, 128), F32), tiles(), field, field, fields(5),
        tiles(STEPS, 8), tiles(STEPS, 8),
        pltpu.VMEM((STEPS, 2, 8, cells), F32), pltpu.VMEM((STEPS, 2, 8, cells), F32),
        pltpu.VMEM((STEPS, 2, 4, lev, 128), F32), pltpu.VMEM((STEPS, 2, 4, lev, 128), F32),
        pltpu.VMEM((2, 3, lev, 128), F32), pltpu.VMEM((2, 3, lev, 128), F32),
        tiles(3), tiles(2, 3),
        tiles(STEPS, 2), tiles(STEPS, 2), tiles(STEPS, 2), tiles(STEPS, 2),
        pltpu.SMEM((rows,), F32), pltpu.SemaphoreType.DMA((10,)),
        pltpu.SemaphoreType.DMA((STEPS, 13)), pltpu.SemaphoreType.DMA((STEPS, 13)),
    ]
    state = pl.pallas_call(
        functools.partial(kernel, n_lon, n_lat, lev),
        out_shape=jax.ShapeDtypeStruct((4, cells, cols), F32),
        in_specs=[hbm] * 10,
        out_specs=vmem,
        scratch_shapes=scratch,
        compiler_params=pltpu.CompilerParams(
            collective_id=0, has_side_effects=True, vmem_limit_bytes=40 * 1024 * 1024
        ),
        name="adjoint",
    )(*[pltpu.with_memory_space_constraint(v, pltpu.HBM) for v in (*flat, flags, sea_mask.reshape(cells, cols), block_inverse, coupling)])
    grads = pl.pallas_call(
        store,
        out_shape=[jax.ShapeDtypeStruct((cells, cols), F32)] * 4,
        in_specs=[anywhere],
        out_specs=[hbm] * 4,
        scratch_shapes=[pltpu.SemaphoreType.DMA((4,))],
        compiler_params=pltpu.CompilerParams(vmem_limit_bytes=8 * 1024 * 1024),
        name="store",
    )(state)
    return tuple(g.reshape(lev, rows, cols) for g in grads)


def solution(mesh):
    field = P("depth", "lat", "lon")
    in_specs = (field,) * 6 + (P(None, "depth", "lat", "lon"), field, P("lat", "depth", None), P("lat"))
    return jax.shard_map(
        functools.partial(on_device, mesh.shape["lon"], mesh.shape["lat"]),
        mesh=mesh,
        in_specs=in_specs,
        out_specs=(field,) * 4,
        check_vma=False,
    )
```

```python
import functools

import jax
import jax.numpy as jnp
from jax import lax
from jax.experimental import pallas as pl
from jax.experimental.pallas import tpu as pltpu
from jax.sharding import PartitionSpec as P

MESH = pl.DeviceIdType.MESH
F32, BF16, I32 = jnp.float32, jnp.bfloat16, jnp.int32

STEPS = 2
advect_scale = 0.25
diffusion = 0.5
gravity = 0.1
pressure_scale = 1.0
viscosity = 0.1
haline = 0.8

CORNER, PLANE, ZU, ZV, ZS = 0, 1, 5, 6, 7
LOW, HIGH = 0, 1
DEP, LON, LAT, DLON, DLAT, COEF, MISC = 0, 1, 3, 5, 7, 9, 11


def tile(k):
    return pl.ds(pl.multiple_of(k * 8, 8), 8)


def split(value):
    high = value.astype(BF16)
    return high, (value - high.astype(F32)).astype(BF16)


def kernel(
    n_lon, n_lat, lev,
    a_t, a_s, a_u, a_v, es_h, ns_h, fl_h, sea_h, inv_h, coup_h,
    out,
    st, es, ns, fl, sea_i, inv,
    sea, cs, sh, e_own, w_own, n_own, s_own, c0, proj, hx, enh, w3,
    wlat, cs_lat, spike, q, pc, m5,
    d_s, d_r, lon_s, lon_r, lat_s, lat_r, coef_s, coef_r, misc_s, misc_r, dl_s, dl_r, dt_s, dt_r,
    coup, in_sem, send_sem, recv_sem,
):
    lon, lat, dep = lax.axis_index("lon"), lax.axis_index("lat"), lax.axis_index("depth")
    edge = (lev - 1) * (1 - dep)
    cells = lev * 8
    east, west = lax.rem(lon + 1, n_lon), lax.rem(lon + n_lon - 1, n_lon)
    has_low, has_high = lat > 0, lat < n_lat - 1
    other = 1 - dep

    barrier = pltpu.get_barrier_semaphore()

    def greet(device):
        pl.semaphore_signal(barrier, inc=1, device_id=device, device_id_type=MESH)

    for depth in (other, dep):
        greet((east, lat, depth))
        greet((west, lat, depth))
        if depth is other:
            greet((lon, lat, other))

        @pl.when(has_low)
        def _():
            greet((lon, lat - 1, depth))

        @pl.when(has_high)
        def _():
            greet((lon, lat + 1, depth))

    loads = []
    for i, (src, dst) in enumerate(
        [(inv_h, inv), (a_t, st.at[0]), (a_s, st.at[1]), (a_u, st.at[2]), (a_v, st.at[3]),
         (sea_h, sea_i), (es_h, es), (ns_h, ns), (fl_h, fl), (coup_h, coup)]
    ):
        copy = pltpu.make_async_copy(src, dst, in_sem.at[i])
        copy.start()
        loads.append(copy)

    lane = lax.broadcasted_iota(I32, (8, 128), 1)
    sub = lax.broadcasted_iota(I32, (8, 128), 0)
    first_lane, last_lane = lane == 0, lane == 127
    first_sub, last_sub = sub == 0, sub == 7
    zero = jnp.zeros((8, 128), F32)

    def to_east(a, halo):
        return jnp.where(last_lane, halo, pltpu.roll(a, 127, 1))

    def to_west(a, halo):
        return jnp.where(first_lane, halo, pltpu.roll(a, 1, 1))

    def to_north(a, halo):
        return jnp.where(last_sub, halo, pltpu.roll(a, 7, 0))

    def to_south(a, halo):
        return jnp.where(first_sub, halo, pltpu.roll(a, 1, 0))

    def copies(step):
        def remote(slot, src, dst, device):
            return pltpu.make_async_remote_copy(
                src_ref=src, dst_ref=dst, send_sem=send_sem.at[step, slot],
                recv_sem=recv_sem.at[step, slot], device_id=device, device_id_type=MESH,
            )

        first = step == 0
        upward = pl.ds(0, 8) if first else pl.ds(1, 6)
        downward = pl.ds(0, 5) if first else pl.ds(1, 4)
        todo = {}
        todo["up"] = (remote(DEP, d_s.at[step, upward], d_r.at[step, upward], (lon, lat, other)), dep == 1, dep == 0)
        todo["down"] = (remote(DEP, d_s.at[step, downward], d_r.at[step, downward], (lon, lat, other)), dep == 0, dep == 1)
        for side in (LOW, HIGH):
            far = 1 - side
            beside = east if side == HIGH else west
            row = lat + 1 if side == HIGH else lat - 1
            sends, gets = (has_high, has_low) if side == HIGH else (has_low, has_high)
            todo["dlon", side] = (remote(DLON + side, dl_s.at[step, side], dl_r.at[step, far], (beside, lat, other)), None, None)
            todo["dlat", side] = (remote(DLAT + side, dt_s.at[step, side], dt_r.at[step, far], (lon, row, other)), sends, gets)
            todo["lon", side] = (remote(LON + side, lon_s.at[step, side], lon_r.at[step, far], (beside, lat, dep)), None, None)
            todo["lat", side] = (remote(LAT + side, lat_s.at[step, side], lat_r.at[step, far], (lon, row, dep)), sends, gets)
            if first:
                count = 3 if side == HIGH else 1
                todo["coef", side] = (
                    remote(COEF + side, coef_s.at[side, pl.ds(0, count)], coef_r.at[far, pl.ds(0, count)], (lon, row, dep)), sends, gets)
                todo["misc", side] = (remote(MISC + side, misc_s, misc_r.at[far], (lon, row, dep)), sends, gets)
        return todo

    def act(entry, what):
        descriptor, sends, gets = entry
        call = {"start": descriptor.start, "send": descriptor.wait_send, "recv": descriptor.wait_recv}[what]
        condition = gets if what == "recv" else sends
        if condition is None:
            call()
        else:
            pl.when(condition)(call)

    for side, missing in ((LOW, lat == 0), (HIGH, lat == n_lat - 1)):

        @pl.when(missing)
        def _():
            for step in range(STEPS):
                lat_r[step, side] = jnp.zeros(lat_r.shape[2:], F32)
                dt_r[step, side] = zero
            coef_r[side] = jnp.zeros(coef_r.shape[1:], F32)
            misc_r[side] = jnp.zeros(misc_r.shape[1:], F32)

    loads[0].wait()
    loads[9].wait()
    coupling = zero
    for y in range(8):
        coupling = jnp.where(sub == y, coup[y], coupling)
    spike[...] = zero
    for y in range(8):
        spike[y : y + 1, 0:lev] = inv[y, pl.ds(edge, 1), :]
        high, low = split(inv[y])
        w3[y] = jnp.concatenate([high, high, low], axis=0)
        at_edge = lax.broadcasted_iota(I32, (lev, lev), 1) == edge
        column = jnp.sum(jnp.where(at_edge, inv[y], 0.0), axis=1, keepdims=True)
        pc[pl.ds(y, lev, stride=8), :] = jnp.broadcast_to(column, (lev, 128))
    spike_rows = spike[...]
    corner = jnp.broadcast_to(
        jnp.sum(jnp.where(lane == edge, spike_rows, 0.0), axis=1, keepdims=True), (8, 128)
    )
    scaled = spike_rows * coupling
    for k in range(lev):
        cs[tile(k)] = jnp.broadcast_to(scaled[:, k : k + 1], (8, 128))
    misc_s[0] = scaled
    misc_s[1] = coupling
    misc_s[2] = corner

    def project(step):
        for y in range(8):
            rows = pl.ds(y, lev, stride=8)
            column = jnp.concatenate([st[f, rows, :] for f in range(4)], axis=1)
            high, low = split(column)
            stacked = jnp.concatenate([high, low, high], axis=0)
            result = lax.dot_general(
                w3[y], stacked, (((0,), (0,)), ((), ())), preferred_element_type=F32
            )
            for f in range(4):
                part = result[:, f * 128 : (f + 1) * 128]
                proj[f, rows, :] = part
                if y == 0:
                    lat_s[step, LOW, f] = part
                if y == 7:
                    lat_s[step, HIGH, f] = part

    for copy in loads[1:5]:
        copy.wait()
    project(0)

    for copy in loads[5:9]:
        copy.wait()

    def prepare(k, carry):
        t = tile(k)
        mask = sea_i[t].astype(F32)
        sea[t] = mask
        quarter = mask * advect_scale
        speed_e, speed_n = es[t], ns[t]
        for n in range(STEPS):
            flag = fl[n, t]
            third = lax.shift_right_logical(flag * 11, 5)
            zonal = (flag - 3 * third).astype(F32) * 0.5
            merid = third.astype(F32) * 0.5
            e_own[n, t] = quarter * (speed_e * (1.0 - zonal) + diffusion)
            w_own[n, t] = quarter * (speed_e * zonal - diffusion)
            n_own[n, t] = quarter * (speed_n * (1.0 - merid) + diffusion)
            s_own[n, t] = quarter * (speed_n * merid - diffusion)
        return carry[0] + mask * cs[t], carry[1] + pc[t]

    spike_sum, pc_sum = lax.fori_loop(0, lev, prepare, (zero, zero), unroll=4)
    d_s[0, CORNER] = corner
    d_s[0, ZS] = spike_sum
    for side, y in ((LOW, 0), (HIGH, 7)):
        rows = pl.ds(y, lev, stride=8)
        coef_s[side, 0] = sea[rows, :]
        if side == HIGH:
            for n in range(STEPS):
                coef_s[side, 1 + n] = s_own[n, rows, :]

    for y in range(8):
        rows = pl.ds(y, lev, stride=8)
        ones = sea[rows, :].astype(BF16)
        high, low = split(inv[y])
        q[rows, :] = jnp.dot(high, ones, preferred_element_type=F32) + jnp.dot(low, ones, preferred_element_type=F32)

    pick_row = lax.broadcasted_iota(I32, (16, 128), 0)
    pick_lane = lax.broadcasted_iota(I32, (16, 128), 1)
    pick_edge = pick_lane == jnp.where(pick_row < 8, 0, 127)

    def first_sums():
        def sums(k, carry):
            t = tile(k)
            return carry[0] + sea[t] * proj[2, t], carry[1] + sea[t] * proj[3, t]

        both = lax.fori_loop(0, lev, sums, (zero, zero), unroll=8)
        return [proj[f, tile(edge)] for f in range(4)] + list(both)

    def messages(step, sent):
        planes, z_u, z_v = list(sent[:4]), sent[4], sent[5]
        for f in range(4):
            d_s[step, PLANE + f] = planes[f]
        d_s[step, ZU] = z_u
        d_s[step, ZV] = z_v
        for side, x in ((LOW, 0), (HIGH, 127)):
            packed = zero
            for i, value in enumerate(planes + [z_u, spike_sum]):
                packed = jnp.where(lane == i, jnp.broadcast_to(value[:, x : x + 1], (8, 128)), packed)
            dl_s[step, side] = packed
        for side, y in ((LOW, 0), (HIGH, 7)):
            for i, value in enumerate([corner] + planes + [z_v, spike_sum]):
                dt_s[step, side, i : i + 1, :] = value[y : y + 1, :]
            dt_s[step, side, 7:8, :] = zero[0:1, :]

    def edges(step):
        fields = [proj.at[f] for f in range(4)]
        if step == 0:
            fields = fields + [sea, w_own.at[0], w_own.at[1]]
        total = jnp.zeros((16, cells), F32)
        for i, field in enumerate(fields):
            pick = jnp.where(pick_edge & (lax.rem(pick_row, 8) == i), 1.0, 0.0).astype(BF16)
            for part in split(field[...]):
                total += lax.dot_general(
                    pick, part, (((1,), (1,)), ((), ())), preferred_element_type=F32
                )
        lon_s[step, LOW] = total[0:8]
        lon_s[step, HIGH] = total[8:16]

    def spread(step):
        count = 7 if step == 0 else 4
        parts = []
        for side in (HIGH, LOW):
            value = lon_r[step, side]
            high = value.astype(BF16).astype(F32)
            parts += [high, value - high]
        stacked = jnp.concatenate(parts, axis=0).astype(BF16)
        row = lax.broadcasted_iota(I32, (32, 128), 0)
        at = lax.broadcasted_iota(I32, (32, 128), 1) == jnp.where(row < 16, 127, 0)
        place = jnp.concatenate(
            [jnp.where(at & (lax.rem(row, 8) == i), 1.0, 0.0) for i in range(count)], axis=1
        ).astype(BF16)
        wide = lax.dot_general(stacked, place, (((0,), (0,)), ((), ())), preferred_element_type=F32)
        for i, field in enumerate([hx.at[0], hx.at[1], hx.at[2], hx.at[3], sh, enh.at[0], enh.at[1]][:count]):
            field[...] = wide[:, i * 128 : (i + 1) * 128]

    def faces(n, k, carry):
        t = tile(k)
        mask, halo = sea[t], sh[t]
        row = pl.ds(k, 1)
        mask_e = to_east(mask, halo)
        mask_n = to_north(mask, coef_r[HIGH, 0, row, :])
        e = e_own[n, t] * mask_e
        w = mask * to_west(w_own[n, t], enh[n, t])
        north = n_own[n, t] * mask_n
        south = mask * to_south(s_own[n, t], coef_r[LOW, 1 + n, row, :])
        e_own[n, t] = e
        w_own[n, t] = w
        n_own[n, t] = north
        s_own[n, t] = south
        c0[n, t] = (1.0 - e + w) - (north - south)
        return carry

    def spread_spikes():
        k_at = lax.broadcasted_iota(I32, (lev, 128), 0)
        same = k_at == lax.broadcasted_iota(I32, (lev, 128), 1)
        for side, y in ((LOW, 7), (HIGH, 0)):
            row = misc_r[side, 0, y : y + 1, :]
            column = jnp.sum(jnp.where(same, jnp.broadcast_to(row, (lev, 128)), 0.0), axis=1, keepdims=True)
            cs_lat[side] = jnp.broadcast_to(column, (lev, 128))

    row_at = (sub + lat * 8).astype(F32)
    coriolis = 0.2 + 0.6 * (row_at + 0.5) / (8.0 * n_lat)

    def masses():
        def level(i, carry):
            k = lev - 1 - i
            t = tile(k)
            row = pl.ds(k, 1)
            here = sea[t] * cs[t]
            side = sh[t] * cs[t]
            values = [
                here, to_east(here, side), to_west(here, side),
                to_north(here, coef_r[HIGH, 0, row, :] * cs_lat[HIGH, row, :]),
                to_south(here, coef_r[LOW, 0, row, :] * cs_lat[LOW, row, :]),
            ]
            for j in range(5):
                m5[j, t] = values[j]
            above, by_plane, by_above, by_mass = carry
            weight, mass = pc[t], q[t]
            return (
                above - weight,
                tuple(c + weight * v for c, v in zip(by_plane, values)),
                tuple(c + above * v for c, v in zip(by_above, values[1:])),
                tuple(c + mass * v for c, v in zip(by_mass, values)),
            )

        return lax.fori_loop(0, lev, level, (pc_sum, (zero,) * 5, (zero,) * 4, (zero,) * 5), unroll=8)[1:]

    half = 0.5 * pressure_scale

    def base(step, n, target):
        for side in (LOW, HIGH):
            for f in range(4):
                wlat[side, f] = coef_r[side, 0] * lat_r[step, side, f]
        count = 11 if step < STEPS - 1 else 0

        def level(i, carry):
            below, sums = carry[0], list(carry[1:])
            k = lev - 1 - i
            t = tile(k)
            row = pl.ds(k, 1)
            mask, halo = sea[t], sh[t]
            w, e_, w_, n_, s_ = [], [], [], [], []
            for f in range(4):
                here = mask * proj[f, t]
                side = halo * hx[f, t]
                w.append(here)
                e_.append(to_east(here, side))
                w_.append(to_west(here, side))
                n_.append(to_north(here, wlat[HIGH, f, row, :]))
                s_.append(to_south(here, wlat[LOW, f, row, :]))
            below = below + half * ((e_[2] - w_[2]) + (n_[3] - s_[3]))
            lift = gravity * below
            coefs = [c0[n, t], e_own[n, t], -w_own[n, t], n_own[n, t], -s_own[n, t]]
            new = [
                (coefs[0] * w[f] + coefs[1] * e_[f]) + (coefs[3] * n_[f] + coefs[2] * w_[f]) + (part + coefs[4] * s_[f])
                for f, part in ((0, lift), (1, -haline * lift))
            ]
            for f, turn in ((2, -coriolis * w[3]), (3, coriolis * w[2])):
                around = (e_[f] + w_[f]) + (n_[f] + s_[f])
                new.append((1.0 - 4.0 * viscosity) * w[f] + turn + viscosity * around)
            for f in range(4):
                target[f, t] = new[f]
            coefs = [c * m5[j, t] for j, c in enumerate(coefs)]
            for ref, c in zip((c0, e_own, w_own, n_own, s_own), coefs):
                ref[n, t] = c
            if sums:
                weight, mass = pc[t], q[t]
                for f in range(4):
                    sums[f] = sums[f] + weight * new[f]
                sums[4] = sums[4] + mass * new[2]
                sums[5] = sums[5] + mass * new[3]
                for j in range(5):
                    sums[6 + j] = sums[6 + j] + weight * coefs[j]
            return (below, *sums)

        return lax.fori_loop(0, lev, level, (zero,) * (1 + count), unroll=4)[1:]

    def carry_over(step):
        other_corner = d_r[0, CORNER]
        alpha = 1.0 / (1.0 - coupling * coupling * corner * other_corner)
        beta = coupling * other_corner * alpha
        gamma = coupling * corner * alpha
        own = [proj[f, tile(edge)] for f in range(4)]
        far = [d_r[step, PLANE + f] for f in range(4)]
        carried = [alpha * far[f] + beta * own[f] for f in range(4)]

        def beside(i):
            low = jnp.broadcast_to(dl_r[step, LOW, :, i : i + 1], (8, 128))
            high = jnp.broadcast_to(dl_r[step, HIGH, :, i : i + 1], (8, 128))
            return jnp.where(last_lane, high, jnp.where(first_lane, low, 0.0))

        own_side = [hx[f, tile(edge)] for f in range(4)]
        far_side = [beside(f) for f in range(4)]
        side = [alpha * far_side[f] + beta * own_side[f] for f in range(4)]

        z_u = d_r[step, ZU] + d_r[0, ZS] * (alpha * own[2] + gamma * far[2])
        z_v = d_r[step, ZV] + d_r[0, ZS] * (alpha * own[3] + gamma * far[3])
        z_side = beside(4) + beside(5) * (alpha * own_side[2] + gamma * far_side[2])
        z_rows, rows = [], []
        for at, y in ((LOW, 7), (HIGH, 0)):
            c = misc_r[at, 1, y : y + 1, :]
            mine = misc_r[at, 2, y : y + 1, :]
            theirs = dt_r[step, at, 0:1, :]
            a = 1.0 / (1.0 - c * c * mine * theirs)
            b = c * theirs * a
            g = c * mine * a
            near = [lat_r[step, at, f, pl.ds(edge, 1), :] for f in range(4)]
            row = [dt_r[step, at, 1 + f : 2 + f, :] for f in range(4)]
            rows.append([a * row[f] + b * near[f] for f in range(4)])
            z_rows.append(dt_r[step, at, 5:6, :] + dt_r[step, at, 6:7, :] * (a * near[3] + g * row[3]))
        deeper = half * (
            (to_east(z_u, z_side) - to_west(z_u, z_side))
            + (to_north(z_v, z_rows[HIGH]) - to_south(z_v, z_rows[LOW]))
        )
        deeper = jnp.where(dep == 0, deeper, 0.0)
        around = [
            (carried[f], to_east(carried[f], side[f]), to_west(carried[f], side[f]),
             to_north(carried[f], rows[HIGH][f]), to_south(carried[f], rows[LOW][f]))
            for f in range(4)
        ]
        turned = (
            (1.0 - 4.0 * viscosity) * carried[2] - coriolis * carried[3],
            (1.0 - 4.0 * viscosity) * carried[3] + coriolis * carried[2],
        )
        slow = [[viscosity * v for v in around[2 + f]] for f in range(2)]
        return around, turned, slow, deeper

    def combine(weights, values):
        terms = [a * b for a, b in zip(weights, values)]
        return (terms[0] + terms[1]) + (terms[2] + terms[3]) + sum(terms[4:], zero)

    def next_sums(sums, weights, interface):
        around, turned, slow, deeper = interface
        by_plane, by_above, by_mass = weights
        press = half * (by_above[0] * around[2][1] - by_above[1] * around[2][2] + by_above[2] * around[3][3] - by_above[3] * around[3][4])
        lift = gravity * (press + pc_sum * deeper)
        out_sums = [
            sums[f] + combine(sums[6:11], around[f]) + part for f, part in ((0, lift), (1, -haline * lift))
        ]
        for f in range(2):
            out_sums.append(sums[2 + f] + combine(by_plane, [turned[f]] + slow[f][1:]))
        for f in range(2):
            out_sums.append(sums[4 + f] + combine(by_mass, [turned[f]] + slow[f][1:]))
        return out_sums

    def finish(n, target, interface):
        around, turned, slow, deeper = interface

        def level(i, below):
            t = tile(lev - 1 - i)
            m = [m5[j, t] for j in range(5)]
            east_u, west_u = m[1] * around[2][1], m[2] * around[2][2]
            north_v, south_v = m[3] * around[3][3], m[4] * around[3][4]
            below = below + half * ((east_u - west_u) + (north_v - south_v))
            lift = gravity * below
            coefs = [c0[n, t], e_own[n, t], w_own[n, t], n_own[n, t], s_own[n, t]]
            target[0, t] = target[0, t] + combine(coefs, around[0]) + lift
            target[1, t] = target[1, t] + combine(coefs, around[1]) - haline * lift
            target[2, t] = (target[2, t] + m[0] * turned[0]) + viscosity * (east_u + west_u) + (m[3] * slow[0][3] + m[4] * slow[0][4])
            target[3, t] = (target[3, t] + m[0] * turned[1]) + viscosity * (north_v + south_v) + (m[1] * slow[1][1] + m[2] * slow[1][2])
            return below

        lax.fori_loop(0, lev, level, deeper, unroll=8)

    messages(0, first_sums())
    edges(0)
    todo = [copies(0), copies(1)]
    pl.semaphore_wait(barrier, 5 + 2 * has_low.astype(I32) + 2 * has_high.astype(I32))

    for step in range(STEPS):
        now = todo[step]
        order = [("dlon", side) for side in (LOW, HIGH)] + ["up", "down"] + [("dlat", side) for side in (LOW, HIGH)]
        if step == 0:
            for name in order:
                act(now[name], "start")
        else:
            project(step)
            edges(step)
        rest = [(kind, side) for kind in ("misc", "coef", "lon", "lat") for side in (LOW, HIGH)]
        for name in rest:
            if name in now:
                act(now[name], "start")
        if step > 0:
            lax.fori_loop(0, lev, functools.partial(faces, STEPS - 1 - step), 0, unroll=8)
        for name in rest[:-2]:
            if name in now:
                act(now[name], "recv")
        spread(step)
        if step == 0:
            spread_spikes()
            lax.fori_loop(0, lev, functools.partial(faces, STEPS - 1), 0, unroll=8)
            weights = masses()
        for name in rest[-2:]:
            act(now[name], "recv")
        n = STEPS - 1 - step
        target = st if step < STEPS - 1 else out
        sums = base(step, n, target)
        for name in order:
            act(now[name], "recv")
        interface = carry_over(step)
        if step < STEPS - 1:
            messages(step + 1, next_sums(sums, weights, interface))
            for name in order:
                act(todo[step + 1][name], "start")
        finish(n, target, interface)
    for now in todo:
        for entry in now.values():
            act(entry, "send")


def store(state, *rest):
    outs, sem = rest[:4], rest[4]
    moves = [pltpu.make_async_copy(state.at[f], outs[f], sem.at[f]) for f in range(4)]
    for move in moves:
        move.start()
    for move in moves:
        move.wait()


def on_device(
    n_lon, n_lat,
    adj_temp, adj_salt, adj_zonal, adj_merid, east_speed, north_speed, branch_flags, sea_mask, block_inverse, coupling,
):
    lev, rows, cols = adj_temp.shape
    cells = lev * rows
    flat = [v.reshape(cells, cols) for v in (adj_temp, adj_salt, adj_zonal, adj_merid, east_speed, north_speed)]
    flags = branch_flags.reshape(STEPS, cells, cols)
    hbm = pl.BlockSpec(memory_space=pltpu.HBM)
    anywhere = pl.BlockSpec(memory_space=pl.ANY)
    vmem = pl.BlockSpec(memory_space=pltpu.VMEM)
    field = pltpu.VMEM((cells, cols), F32)

    def fields(*lead):
        return pltpu.VMEM((*lead, cells, cols), F32)

    def tiles(*lead):
        return pltpu.VMEM((*lead, 8, 128), F32)

    scratch = [
        fields(4), field, field, pltpu.VMEM((STEPS, cells, cols), I32), pltpu.VMEM((cells, cols), I32),
        pltpu.VMEM((rows, lev, lev), F32),
        field, field, field,
        fields(STEPS), fields(STEPS), fields(STEPS), fields(STEPS), fields(STEPS),
        fields(4), fields(4), fields(STEPS), pltpu.VMEM((rows, 3 * lev, lev), BF16),
        pltpu.VMEM((2, 4, lev, 128), F32), pltpu.VMEM((2, lev, 128), F32), tiles(), field, field, fields(5),
        tiles(STEPS, 8), tiles(STEPS, 8),
        pltpu.VMEM((STEPS, 2, 8, cells), F32), pltpu.VMEM((STEPS, 2, 8, cells), F32),
        pltpu.VMEM((STEPS, 2, 4, lev, 128), F32), pltpu.VMEM((STEPS, 2, 4, lev, 128), F32),
        pltpu.VMEM((2, 3, lev, 128), F32), pltpu.VMEM((2, 3, lev, 128), F32),
        tiles(3), tiles(2, 3),
        tiles(STEPS, 2), tiles(STEPS, 2), tiles(STEPS, 2), tiles(STEPS, 2),
        pltpu.SMEM((rows,), F32), pltpu.SemaphoreType.DMA((10,)),
        pltpu.SemaphoreType.DMA((STEPS, 13)), pltpu.SemaphoreType.DMA((STEPS, 13)),
    ]
    state = pl.pallas_call(
        functools.partial(kernel, n_lon, n_lat, lev),
        out_shape=jax.ShapeDtypeStruct((4, cells, cols), F32),
        in_specs=[hbm] * 10,
        out_specs=vmem,
        scratch_shapes=scratch,
        compiler_params=pltpu.CompilerParams(
            collective_id=0, has_side_effects=True, vmem_limit_bytes=40 * 1024 * 1024
        ),
        name="adjoint",
    )(*[pltpu.with_memory_space_constraint(v, pltpu.HBM) for v in (*flat, flags, sea_mask.reshape(cells, cols), block_inverse, coupling)])
    grads = pl.pallas_call(
        store,
        out_shape=[jax.ShapeDtypeStruct((cells, cols), F32)] * 4,
        in_specs=[anywhere],
        out_specs=[hbm] * 4,
        scratch_shapes=[pltpu.SemaphoreType.DMA((4,))],
        compiler_params=pltpu.CompilerParams(vmem_limit_bytes=8 * 1024 * 1024),
        name="store",
    )(state)
    return tuple(g.reshape(lev, rows, cols) for g in grads)


def solution(mesh):
    field = P("depth", "lat", "lon")
    in_specs = (field,) * 6 + (P(None, "depth", "lat", "lon"), field, P("lat", "depth", None), P("lat"))
    return jax.shard_map(
        functools.partial(on_device, mesh.shape["lon"], mesh.shape["lat"]),
        mesh=mesh,
        in_specs=in_specs,
        out_specs=(field,) * 4,
        check_vma=False,
    )
```
